128 devices in a mesh: dp: 16 (over y, x), mp: 8 (over z, core).
Axes of the slice: x: 4, y: 4, z: 4, core: 2. Of those that a mesh axis runs over, the one named last changes fastest.
Arguments:
- inputs: bfloat16 [2, 2048, 2048], P(None, 'dp', 'mp'), may hold values from -6 to 6
- cotangent: bfloat16 [2, 2048, 2048], P(None, 'dp', 'mp'), may hold values from -6 to 6
- row_split: int32 [2], replicated, may hold values from 512 to 1536
- first_gain: bfloat16 [2048], P('mp'), may hold values from 0.5 to 1.5
- branch_weight: bfloat16 [2048, 2816], P('dp', 'mp'), may hold values from -0.125 to 0.125
- value_weight: bfloat16 [2048, 2816], P('dp', 'mp'), may hold values from -0.125 to 0.125
- conv_weight: bfloat16 [4, 16, 176], P(None, 'mp'), may hold values from -3 to 3
- conv_bias: bfloat16 [16, 176], P('mp'), may hold values from -2 to 2
- rate_blocks: bfloat16 [16, 176, 176], P('mp'), may hold values from -0.4375 to 0.4375
- input_blocks: bfloat16 [16, 176, 176], P('mp'), may hold values from -0.4375 to 0.4375
- rate_bias: bfloat16 [16, 176], P('mp'), may hold values from -4 to 4
- input_bias: bfloat16 [16, 176], P('mp'), may hold values from -4 to 4
- decay_param: bfloat16 [16, 176], P('mp'), may hold values from -13 to -4
- out_weight: bfloat16 [2816, 2048], P('mp', 'dp'), may hold values from -0.3125 to 0.3125
- second_gain: bfloat16 [2048], P('mp'), may hold values from 0.5 to 1.5
- gate_weight: bfloat16 [2048, 6144], P('dp', 'mp'), may hold values from -0.125 to 0.125
- up_weight: bfloat16 [2048, 6144], P('dp', 'mp'), may hold values from -0.125 to 0.125
- down_weight: bfloat16 [6144, 2048], P('mp', 'dp'), may hold values from -0.15625 to 0.15625
Outputs:
- layer_out: bfloat16 [2, 2048, 2048], P(None, 'dp', 'mp')
- input_grad: float32 [2, 2048, 2048], P(None, 'dp', 'mp')
- first_gain_grad: float32 [2048], P(('mp', 'dp'))
- branch_weight_grad: float32 [2048, 2816], P('dp', 'mp')
- value_weight_grad: float32 [2048, 2816], P('dp', 'mp')
- conv_weight_grad: float32 [4, 16, 176], P(None, 'mp', 'dp')
- conv_bias_grad: float32 [16, 176], P('mp', 'dp')
- rate_blocks_grad: float32 [16, 176, 176], P('mp', 'dp')
- input_blocks_grad: float32 [16, 176, 176], P('mp', 'dp')
- rate_bias_grad: float32 [16, 176], P('mp', 'dp')
- input_bias_grad: float32 [16, 176], P('mp', 'dp')
- decay_param_grad: float32 [16, 176], P('mp', 'dp')
- out_weight_grad: float32 [2816, 2048], P('mp', 'dp')
- second_gain_grad: float32 [2048], P(('mp', 'dp'))
- gate_weight_grad: float32 [2048, 6144], P('dp', 'mp')
- up_weight_grad: float32 [2048, 6144], P('dp', 'mp')
- down_weight_grad: float32 [6144, 2048], P('mp', 'dp')
The draws below stay inside these ranges and needn't reach their ends.
Inputs may be any that keep to these rules, and one draw needn't show every extreme that they name: row_split leaves each of a micro-batch's two rows at least 1024 tokens, or a quarter of 2048 where that is less.
All inputs are finite; a program needn't handle non-finite values.
Results may differ from the reference program's by a relative error of at most 0.02.
Values may be sent and summed in bfloat16 or wider, within the bound.
No kernel may reach another device: no remote copies, remote signals or barrier semaphores. Data moves between devices by JAX's collectives and lax.ppermute only.
A program may use at most 192 MiB of HBM per device.

```python
import math
from functools import partial
import jax
import jax.numpy as jnp
from jax import lax

D = 2048
FF = 6144
NB = 16
BLK = 176
R = 2816
CONV = 4
MB = 2
MIN_ROW = 1024
TOKENS = 2048


def draw_decay_param(key, part):
    key = jax.random.fold_in(key, 11)
    pick_key, slow_key, fast_key = jax.random.split(key, 3)
    shape = (NB, BLK)
    slow = jnp.exp(jax.random.uniform(slow_key, shape, jnp.float32, math.log(0.05 / TOKENS), math.log(0.4 / TOKENS)))
    fast = jnp.exp(jax.random.uniform(fast_key, shape, jnp.float32, math.log(0.004), math.log(0.012)))
    share = 0.5
    chosen = jax.random.uniform(pick_key, shape, jnp.float32) < share
    rate_value = jnp.where(chosen, slow, fast)
    return jnp.log(jnp.expm1(rate_value)).astype(jnp.bfloat16)


def block_levels(key, dims, cuts, smallest, top_value):
    loudness = 1.0
    for position, shards_of in cuts:
        heights = jax.random.uniform(jax.random.fold_in(jax.random.fold_in(key, 6), position), (shards_of,), jnp.float32, smallest / len(cuts), top_value / len(cuts))
        loudness = loudness * jnp.repeat(jnp.exp(heights), dims[position] // shards_of).reshape((-1,) + (1,) * (len(dims) - 1 - position))
    return loudness


def noise(key, shape, spread, limit, cuts=(), dtype=jnp.bfloat16):
    values = spread * jax.random.normal(key, shape, jnp.float32)
    if cuts:
        values = values * block_levels(key, shape, cuts, -0.22, 0.18)
    return jnp.clip(values, -limit, limit).astype(dtype)


def setup_inputs(seed: int = 0) -> dict:
    splits = jax.random.split(jax.random.key(seed), 19)
    return {
        "inputs": noise(splits[0], (MB, TOKENS, D), 1.0, 6.0, ((1, 16), (2, 8))),
        "cotangent": noise(splits[1], (MB, TOKENS, D), 1.0, 6.0, ((1, 16), (2, 8))),
        "row_split": jax.random.randint(splits[2], (MB,), min(MIN_ROW, TOKENS // 4), TOKENS - min(MIN_ROW, TOKENS // 4) + 1).astype(jnp.int32),
        "first_gain": jnp.clip(1.0 + 0.1 * jax.random.normal(splits[3], (D,), jnp.float32), 0.5, 1.5).astype(jnp.bfloat16),
        "branch_weight": noise(splits[4], (D, R), D ** -0.5, 0.125, ((0, 16), (1, 8))),
        "value_weight": noise(splits[5], (D, R), D ** -0.5, 0.125, ((0, 16), (1, 8))),
        "conv_weight": noise(splits[6], (CONV, NB, BLK), 0.5, 3.0, ((1, 8),)),
        "conv_bias": noise(splits[7], (NB, BLK), 0.3, 2.0, ((0, 8),)),
        "rate_blocks": noise(splits[8], (NB, BLK, BLK), BLK ** -0.5, 0.4375, ((0, 8),)),
        "input_blocks": noise(splits[9], (NB, BLK, BLK), BLK ** -0.5, 0.4375, ((0, 8),)),
        "rate_bias": noise(splits[10], (NB, BLK), 1.0, 4.0, ((0, 8),)),
        "input_bias": noise(splits[11], (NB, BLK), 1.0, 4.0, ((0, 8),)),
        "decay_param": draw_decay_param(jax.random.fold_in(splits[18], 71), 0),
        "out_weight": noise(splits[13], (R, D), (R // 8) ** -0.5, 0.3125, ((0, 8), (1, 16))),
        "second_gain": jnp.clip(1.0 + 0.1 * jax.random.normal(splits[14], (D,), jnp.float32), 0.5, 1.5).astype(jnp.bfloat16),
        "gate_weight": noise(splits[15], (D, FF), D ** -0.5, 0.125, ((0, 16), (1, 8))),
        "up_weight": noise(splits[16], (D, FF), D ** -0.5, 0.125, ((0, 16), (1, 8))),
        "down_weight": noise(splits[17], (FF, D), (FF // 4) ** -0.5, 0.15625, ((0, 8), (1, 16))),
    }


HIGH = lax.Precision.HIGHEST
EPS = 1e-06

@jax.custom_vjp
def low(v):
    return lax.optimization_barrier(v.astype(jnp.bfloat16)).astype(jnp.float32)

@jax.custom_vjp
def low_back(v):
    return v

def low_keep(v):
    return (low(v), None)

def low_pass(kept, grad):
    return (grad,)

def back_keep(v):
    return (v, None)

def back_low(kept, grad):
    return (low(grad),)
low.defvjp(low_keep, low_pass)
low_back.defvjp(back_keep, back_low)

def link(earlier, later):
    return (earlier[0] * later[0], later[0] * earlier[1] + later[1])

def row_masks(places, split_at, conv_span):
    conv_masks = []
    for conv_step in range(conv_span):
        back_pos = places - conv_step
        same_row = ((back_pos >= split_at) == (places >= split_at)) & (back_pos >= 0)
        conv_masks.append(same_row.astype(jnp.float32)[:, None])
    return conv_masks

def convolve(extended, weight, bias_row, conv_masks):
    conv_span = weight.shape[0]
    tok_count = extended.shape[0] - conv_span + 1
    running = jnp.zeros((tok_count, weight.shape[1]), jnp.float32) + bias_row
    for conv_step in range(conv_span):
        offset = conv_span - 1 - conv_step
        running = running + weight[conv_step] * extended[offset:offset + tok_count] * conv_masks[conv_step]
    return running

def gate_terms(rate_pre, input_pre, conv_out, decay_row, keep_mask):
    rate_gate = jax.nn.sigmoid(rate_pre)
    input_gate = jax.nn.sigmoid(input_pre)
    log_decay = -8.0 * jax.nn.softplus(decay_row) * rate_gate
    decay_factor = jnp.exp(log_decay) * keep_mask
    scaled = keep_mask * jnp.sqrt(-jnp.expm1(2.0 * log_decay)) + (1.0 - keep_mask)
    return (decay_factor, scaled * input_gate * conv_out)

def blockwise(act_rows, blocks):
    tok_count = act_rows.shape[0]
    block_count, block_size = (blocks.shape[0], blocks.shape[1])
    shaped = act_rows.reshape(tok_count, block_count, block_size)
    return jnp.einsum('tnb,nbc->tnc', shaped, blocks, precision=HIGH).reshape(tok_count, block_count * block_size)

def rms_scale(act_rows):
    return lax.rsqrt(lax.optimization_barrier(jnp.mean(act_rows * act_rows, axis=1, keepdims=True)) + EPS)

def layer(split_at, act_rows, first_gain, branch_weight, value_weight, conv_weight, conv_bias, rate_blocks, input_blocks, rate_bias, input_bias, decay_param, out_weight, second_gain, gate_weight, up_weight, down_weight):
    tok_count = act_rows.shape[0]
    conv_span = conv_weight.shape[0]
    lane_count = rate_bias.shape[0] * rate_bias.shape[1]
    places = lax.iota(jnp.int32, tok_count)
    keep_mask = (places != split_at).astype(jnp.float32)[:, None]
    conv_masks = row_masks(places, split_at, conv_span)
    normed_one = low(act_rows * rms_scale(act_rows) * first_gain)
    branch_pre = low_back(jnp.dot(normed_one, branch_weight, precision=HIGH))
    branch = jax.nn.gelu(branch_pre)
    value_pre = low_back(jnp.dot(normed_one, value_weight, precision=HIGH))
    extended = jnp.concatenate([jnp.zeros((conv_span - 1, lane_count), jnp.float32), value_pre], axis=0)
    conv_out = low(convolve(extended, conv_weight.reshape(conv_span, lane_count), conv_bias.reshape(lane_count), conv_masks))
    rate_pre = low_back(blockwise(conv_out, rate_blocks) + rate_bias.reshape(lane_count))
    input_pre = low_back(blockwise(conv_out, input_blocks) + input_bias.reshape(lane_count))
    decay_factor, drive_term = gate_terms(rate_pre, input_pre, conv_out, decay_param.reshape(lane_count), keep_mask)
    rnn_state = lax.associative_scan(link, (decay_factor, drive_term))[1]
    mixed_rows = low(rnn_state * branch)
    middle = act_rows + low_back(jnp.dot(mixed_rows, out_weight, precision=HIGH))
    normed_two = low(middle * rms_scale(middle) * second_gain)
    gate_pre = low_back(jnp.dot(normed_two, gate_weight, precision=HIGH))
    up_pre = low_back(jnp.dot(normed_two, up_weight, precision=HIGH))
    hidden = low(jax.nn.gelu(gate_pre) * up_pre)
    return middle + low_back(jnp.dot(hidden, down_weight, precision=HIGH))

def reference(inputs, cotangent, row_split, first_gain, branch_weight, value_weight, conv_weight, conv_bias, rate_blocks, input_blocks, rate_bias, input_bias, decay_param, out_weight, second_gain, gate_weight, up_weight, down_weight):
    params = tuple((item.astype(jnp.float32) for item in (first_gain, branch_weight, value_weight, conv_weight, conv_bias, rate_blocks, input_blocks, rate_bias, input_bias, decay_param, out_weight, second_gain, gate_weight, up_weight, down_weight)))
    outputs = []
    input_grads = []
    totals = None
    for micro_index in range(MB):
        forward = partial(layer, row_split[micro_index])
        result, pull = jax.vjp(forward, inputs[micro_index].astype(jnp.float32), *params)
        grads = pull(cotangent[micro_index].astype(jnp.float32))
        outputs.append(result.astype(jnp.bfloat16))
        input_grads.append(grads[0])
        if totals is None:
            totals = grads[1:]
        else:
            totals = tuple((first_op + second_op for first_op, second_op in zip(totals, grads[1:])))
    return (jnp.stack(outputs), jnp.stack(input_grads), totals[0], totals[1], totals[2], totals[3], totals[4], totals[5], totals[6], totals[7], totals[8], totals[9], totals[10], totals[11], totals[12], totals[13], totals[14])
```

```python
import functools
import math

import jax
import jax.numpy as jnp
from jax import lax
from jax.experimental import pallas as pl
from jax.experimental.pallas import tpu as pltpu
from jax.sharding import PartitionSpec as P

EPS = 1e-06
F32 = jnp.float32
BF16 = jnp.bfloat16
NT = (((1,), (1,)), ((), ()))
TN = (((0,), (0,)), ((), ()))
HALO = 16
SIDE = 4
VMEM_BYTES = 56 * 1024 * 1024
FLOPS_PER_US = 1.15e9
COST_US = {
    "norm_one": 3.5, "rec_fwd": 8.4, "rec_out": 3.7, "ffn": 12.9, "ffn_grad_one": 5.0, "ffn_grad_two": 0.3,
    "ffn_grad_three": 6.3, "ffn_out": 15.0, "dn2_sum": 0.3, "rec_bwd": 0.3, "early_grad": 0.3,
    "early_out": 1.7,
    "gate_bwd": 3.9, "conv_bwd": 5.7, "late_grad": 0.3, "finish": 2.8, "small_out": 1.5, "late_out": 2.5,
}
GELU_K = math.sqrt(2.0 / math.pi)


def mm(a, b):
    return jnp.dot(a, b, preferred_element_type=F32)


def mm_nt(a, b):
    return lax.dot_general(a, b, NT, preferred_element_type=F32)


def mm_tn(a, b):
    return lax.dot_general(a, b, TN, preferred_element_type=F32)


def gelu_pair(x):
    t = jnp.tanh(GELU_K * (x + 0.044715 * (x * x * x)))
    half = 0.5 * (1.0 + t)
    slope = half + 0.5 * x * (1.0 - t * t) * (GELU_K * (1.0 + 0.134145 * (x * x)))
    return x * half, slope


def neg_expm1(x):
    near = jnp.maximum(x, -0.5)
    series = 1.0 / 40320.0 + near * (1.0 / 362880.0)
    for denom in (5040.0, 720.0, 120.0, 24.0, 6.0, 2.0, 1.0):
        series = 1.0 / denom + near * series
    return jnp.where(x > -0.5, -near * series, 1.0 - jnp.exp(x))


def rolled(x, by):
    return x if by == 0 else jnp.roll(x, by, axis=0)


def shift_down(x, step, fill):
    rows = lax.broadcasted_iota(jnp.int32, x.shape, 0)
    return jnp.where(rows < step, fill, jnp.roll(x, step, axis=0))


def shift_up(x, step, fill):
    count = x.shape[0]
    rows = lax.broadcasted_iota(jnp.int32, x.shape, 0)
    return jnp.where(rows >= count - step, fill, jnp.roll(x, -step, axis=0))


def scan_down(a, u):
    step = 1
    while step < a.shape[0]:
        u = u + a * shift_down(u, step, 0.0)
        a = a * shift_down(a, step, 1.0)
        step *= 2
    return a, u


def scan_up(a, u):
    step = 1
    while step < a.shape[0]:
        u = u + a * shift_up(u, step, 0.0)
        a = a * shift_up(a, step, 1.0)
        step *= 2
    return a, u


def conv_mask(place, split_at, back):
    behind = place - back
    return ((behind >= split_at) == (place >= split_at)) & (behind >= 0)


def call(kernel, outs, ins, args, grid=None, out_specs=None, scratch=(), name=None, ties=()):
    kwargs = {}
    if ties:
        count, inner = len(args), kernel

        def kernel(*refs):
            inner(*refs[:count], *refs[count + len(ties) :])

        ins = list(ins) + [pl.BlockSpec(memory_space=pl.ANY)] * len(ties)
        args = tuple(args) + tuple(ties)
    if grid is not None:
        kwargs["grid"] = grid
    return pl.pallas_call(
        kernel,
        out_shape=outs,
        in_specs=ins,
        out_specs=out_specs if out_specs is not None else [WHOLE] * len(outs),
        scratch_shapes=list(scratch),
        compiler_params=pltpu.CompilerParams(vmem_limit_bytes=VMEM_BYTES),
        cost_estimate=pl.CostEstimate(flops=int(COST_US[name] * FLOPS_PER_US), bytes_accessed=0, transcendentals=0),
        name=name,
        **kwargs,
    )(*args)


WHOLE = pl.BlockSpec(memory_space=pltpu.VMEM)
SCALARS = pl.BlockSpec(memory_space=pltpu.SMEM)
ME, ROW_Y, COL_X, DEEP_Z, CORE = 2, 3, 4, 5, 6
NEAR = (0, -1, 1)


def shape(dims, dtype=F32):
    return jax.ShapeDtypeStruct(dims, dtype)


def lane_block(index, width):
    return pl.ds(pl.multiple_of(index * width, width), width)


def lay_parts(s_ref, three, far, three_other, far_other, put):
    z, core = s_ref[DEEP_Z], s_ref[CORE]
    for held, held_far, which in ((three, far, core), (three_other, far_other, 1 - core)):
        for k, dz in enumerate(NEAR):
            put((z + dz + SIDE) % SIDE * 2 + which, held[k])
        put((z + 2) % SIDE * 2 + which, held_far[...])


def norm_one_kernel(s_ref, three, far, three_other, far_other, n1_ref, own_ref, rho_ref, gain_ref, x_ref):
    rows = three.shape[1] - HALO
    width = three.shape[2]
    full = x_ref.shape[1]

    def put(block, value):
        here = lane_block(block, width)
        x_ref[:, here] = value[:rows]
        gain_ref[:, here] = value[rows:].astype(F32)

    lay_parts(s_ref, three, far, three_other, far_other, put)
    total = jnp.zeros((rows, 1), F32)
    for j in range(full // width):
        xj = x_ref[:, j * width : (j + 1) * width].astype(F32)
        total = total + jnp.sum(xj * xj, axis=1, keepdims=True)
    rho = lax.rsqrt(total / full + EPS)
    rho_ref[...] = rho
    batches = own_ref.shape[0] // (rows // 2 - HALO)
    ext = rows // batches
    toks = ext - HALO
    for j in range(full // width):
        here = slice(j * width, (j + 1) * width)
        n1 = (x_ref[:, here].astype(F32) * rho * gain_ref[0:1, here]).astype(BF16)
        n1_ref[:, here] = n1
        for m in range(batches):
            own_ref[m * toks : (m + 1) * toks, here] = n1[m * ext + HALO : (m + 1) * ext]


def rec_fwd_kernel(s_ref, n1_ref, shards_ref, vec_ref, wr_ref, wi_ref,
                   w_ref, yb_ref, vb_ref, c_ref, r_ref, i_ref, a_ref, pr_ref, st_ref, last_ref):
    batches = 2
    ext = n1_ref.shape[0] // batches
    toks = ext - HALO
    lanes = vec_ref.shape[1]
    piece = shards_ref.shape[2]
    for i in range(shards_ref.shape[0]):
        w_ref[:, i * piece : (i + 1) * piece] = shards_ref[i]
    start = s_ref[ME] * toks
    vb_ref[...] = mm_nt(n1_ref[...], w_ref[lanes : 2 * lanes])
    last_ref[...] = jnp.zeros_like(last_ref)
    for m in range(batches):
        own = slice(m * toks, (m + 1) * toks)
        yb_ref[own] = mm_nt(n1_ref[m * ext + HALO : (m + 1) * ext], w_ref[:lanes])
        vb = vb_ref[m * ext : (m + 1) * ext]
        place = start + lax.broadcasted_iota(jnp.int32, (toks, lanes), 0)
        split_at = s_ref[m]
        conv = jnp.zeros((toks, lanes), F32) + vec_ref[4:5]
        for k in range(4):
            term = vec_ref[k : k + 1] * rolled(vb, k)[HALO:]
            conv = conv + jnp.where(conv_mask(place, split_at, k), term, 0.0)
        c16 = conv.astype(BF16)
        c = c16.astype(F32)
        rate = jax.nn.sigmoid(mm(c16, wr_ref[...]) + vec_ref[5:6])
        gate = jax.nn.sigmoid(mm(c16, wi_ref[...]) + vec_ref[6:7])
        la = -vec_ref[7:8] * rate
        keep = (place != split_at).astype(F32)
        a = keep * jnp.exp(la)
        u = (keep * jnp.sqrt(neg_expm1(2.0 * la)) + (1.0 - keep)) * gate * c
        c_ref[own] = c16
        r_ref[own] = rate
        i_ref[own] = gate
        a_ref[own] = a
        prod, state = scan_down(a, u)
        pr_ref[own] = prod
        st_ref[own] = state
        last_ref[2 * m : 2 * m + 1] = prod[toks - 1 :]
        last_ref[2 * m + 1 : 2 * m + 2] = state[toks - 1 :]


def carry_of(s_ref, all_ref, m, backward):
    me = s_ref[ME]
    count = all_ref.shape[0]
    carry = jnp.zeros((1, all_ref.shape[2]), F32)
    for q in range(count - 1, 0, -1) if backward else range(count - 1):
        longer = all_ref[q, 2 * m : 2 * m + 1] * carry + all_ref[q, 2 * m + 1 : 2 * m + 2]
        carry = jnp.where((q > me) if backward else (q < me), longer, carry)
    return carry


def chunk_places(s_ref):
    z, core = s_ref[DEEP_Z], s_ref[CORE]
    for r in range(SIDE):
        yield r, (z + r) % SIDE * 2 + core, (z + r) % SIDE * 2 + 1 - core


def rec_out_kernel(s_ref, all_ref, pr_ref, st_ref, yb_ref, w_ref,
                   h_ref, carry_ref, o_ref, keep_ref, swap_ref):
    batches = 2
    toks = pr_ref.shape[0] // batches
    carry_ref[...] = jnp.zeros_like(carry_ref)
    for m in range(batches):
        own = slice(m * toks, (m + 1) * toks)
        carry = carry_of(s_ref, all_ref, m, False)
        carry_ref[m : m + 1] = carry
        h = st_ref[own] + pr_ref[own] * carry
        h_ref[own] = h
        o_ref[own] = (h * gelu_pair(yb_ref[own])[0]).astype(BF16)
    width = keep_ref.shape[2]
    for r, mine, other in chunk_places(s_ref):
        swap_ref[r] = mm(o_ref[...], w_ref[:, lane_block(other, width)]).astype(BF16)
        keep_ref[r] = mm(o_ref[...], w_ref[:, lane_block(mine, width)]).astype(BF16)


def inner_rows(products):
    ones = jnp.ones((HALO, products.shape[1]), F32)
    sums = lax.dot_general(ones, products, NT, precision=lax.Precision.HIGHEST, preferred_element_type=F32)
    high = sums.astype(BF16)
    low = (sums - high.astype(F32)).astype(BF16)
    rows = lax.broadcasted_iota(jnp.int32, sums.shape, 0)
    return jnp.where(rows == 0, high.astype(F32), jnp.where(rows == 1, low.astype(F32), 0.0)).astype(BF16)


def ffn_kernel(s_ref, three, far, three_other, far_other, c3_ref, cf_ref, c3o_ref, cfo_ref, gain_ref, w_ref,
               n2_ref, x2_ref, rho_ref, cotf_ref, hid_ref, dgt_ref, dup_ref, po_ref, keep_ref, swap_ref,
               acc_o, acc_d, acc_i):
    step = pl.program_id(0)
    deep, _, rows, cols = w_ref.shape
    _, toks, width = three.shape
    parts = x2_ref.shape[1] // width

    @pl.when(step == 0)
    def _():
        def put(block, value):
            x2_ref[:, lane_block(block, width)] = value

        def put_cot(block, value):
            cotf_ref[:, lane_block(block, width)] = value

        lay_parts(s_ref, three, far, three_other, far_other, put)
        lay_parts(s_ref, c3_ref, cf_ref, c3o_ref, cfo_ref, put_cot)
        total = jnp.zeros((toks, 1), F32)
        for j in range(parts):
            here = slice(j * width, (j + 1) * width)
            xj = x2_ref[:, here].astype(F32)
            total = total + jnp.sum(xj * xj, axis=1, keepdims=True)
        rho = lax.rsqrt(total / (parts * width) + EPS)
        rho_ref[...] = rho
        for j in range(parts):
            here = slice(j * width, (j + 1) * width)
            n2_ref[:, here] = (x2_ref[:, here].astype(F32) * rho * gain_ref[1:2, here]).astype(BF16)
        acc_o[...] = jnp.zeros_like(acc_o)
        acc_d[...] = jnp.zeros_like(acc_d)
        acc_i[...] = jnp.zeros_like(acc_i)

    wg = w_ref[:, 0].reshape(deep * rows, cols)
    wu = w_ref[:, 1].reshape(deep * rows, cols)
    wd = w_ref[:, 2].reshape(deep * rows, cols)
    gt = mm(n2_ref[...], wg)
    up = mm(n2_ref[...], wu)
    dm = mm(cotf_ref[...], wd)
    act, slope = gelu_pair(gt)
    hid = (act * up).astype(BF16)
    dgt = (slope * up * dm).astype(BF16)
    dup = (act * dm).astype(BF16)
    hid_ref[...] = hid
    dgt_ref[...] = dgt
    dup_ref[...] = dup
    acc_i[...] += dgt.astype(F32) * gt + dup.astype(F32) * up
    acc_o[...] += mm_nt(hid, wd)
    acc_d[...] += mm_nt(dgt, wg) + mm_nt(dup, wu)

    @pl.when(step == pl.num_programs(0) - 1)
    def _():
        side = inner_rows(acc_i[...])
        po_ref[...] = acc_o[...].astype(BF16)
        core = s_ref[CORE]
        for z in range(SIDE):
            for ref, block in ((swap_ref, 2 * z + 1 - core), (keep_ref, 2 * z + core)):
                ref[z, :toks] = acc_d[:, lane_block(block, width)].astype(BF16)
                ref[z, toks:] = side


def rec_bwd_kernel(s_ref, dn2_ref, other_ref, x2_ref, cotf_ref, gain_ref, rho_ref, inner_ref, w_ref,
                   yb_ref, h_ref, a_ref, pr_ref,
                   gr_ref, dyb_ref, la_ref, lp_ref, first_ref):
    width = dn2_ref.shape[2]
    full = x2_ref.shape[1]
    batches = 2
    toks = x2_ref.shape[0] // batches
    rho = rho_ref[...]
    back = rho * rho * rho / full * inner_ref[...]

    core = s_ref[CORE]
    for z in range(SIDE):
        for ref, block in ((dn2_ref, 2 * z + core), (other_ref, 2 * z + 1 - core)):
            here = lane_block(block, width)
            gx2 = (cotf_ref[:, here].astype(F32) + rho * gain_ref[1:2, here] * ref[z].astype(F32)
                   - x2_ref[:, here].astype(F32) * back)
            gr_ref[:, here] = gx2.astype(BF16)
    do = mm_nt(gr_ref[...], w_ref[...])
    ends = []
    for m in range(batches):
        own = slice(m * toks, (m + 1) * toks)
        act, slope = gelu_pair(yb_ref[own])
        dom = do[own]
        dyb_ref[own] = (slope * h_ref[own] * dom).astype(BF16)
        a = a_ref[own]
        prod, adj = scan_up(shift_up(a, 1, 1.0), dom * act)
        la_ref[own] = adj
        lp_ref[own] = prod
        ends += [pr_ref[(m + 1) * toks - 1 : (m + 1) * toks], a[0:1] * adj[0:1]]
    ends = jnp.concatenate(ends + [jnp.zeros_like(ends[0])] * (first_ref.shape[1] - len(ends)), axis=0)
    for i in range(first_ref.shape[0]):
        first_ref[i] = ends


def gate_bwd_kernel(s_ref, all_ref, la_ref, lp_ref, a_ref, h_ref, carry_ref, c_ref, r_ref,
                    i_ref, vec_ref, wr_ref, wi_ref, dza_ref, dzx_ref, dc_ref, head_ref, sums_ref):
    batches = 2
    toks = la_ref.shape[0] // batches
    lanes = la_ref.shape[1]
    start = s_ref[ME] * toks
    lam = vec_ref[7:8]
    acc = [jnp.zeros((1, lanes), F32) for _ in range(3)]
    for m in range(batches):
        own = slice(m * toks, (m + 1) * toks)
        q = la_ref[own] + lp_ref[own] * carry_of(s_ref, all_ref, m, True)
        rows = lax.broadcasted_iota(jnp.int32, (toks, lanes), 0)
        keep = (start + rows != s_ref[m]).astype(F32)
        hprev = jnp.where(rows == 0, carry_ref[m : m + 1], jnp.roll(h_ref[own], 1, axis=0))
        rate = r_ref[own]
        gate = i_ref[own]
        c = c_ref[own].astype(F32)
        la = -lam * rate
        root = jnp.sqrt(neg_expm1(2.0 * la))
        decay = jnp.exp(la)
        scaled = keep * root + (1.0 - keep)
        dla = q * hprev * keep * decay - q * keep * gate * c * (decay * decay / root)
        dza = (dla * (-lam) * rate * (1.0 - rate)).astype(BF16)
        dc0 = q * scaled * gate
        dzx = (dc0 * c * (1.0 - gate)).astype(BF16)
        dza_ref[own] = dza
        dzx_ref[own] = dzx
        dc = dc0 + mm_nt(dza, wr_ref[...]) + mm_nt(dzx, wi_ref[...])
        dc_ref[own] = dc
        head_ref[m] = dc[0:8]
        acc[0] += jnp.sum(dza.astype(F32), axis=0, keepdims=True)
        acc[1] += jnp.sum(dzx.astype(F32), axis=0, keepdims=True)
        acc[2] += jnp.sum(dla * rate, axis=0, keepdims=True)
    sums_ref[...] = jnp.zeros_like(sums_ref)
    sums_ref[0:1] = acc[0]
    sums_ref[1:2] = acc[1]
    sums_ref[2:3] = -acc[2] * vec_ref[8:9]


def conv_bwd_kernel(s_ref, dc_ref, head_ref, vb_ref, yb_ref, dyb_ref, vec_ref, w_ref,
                    dvb_ref, keep_ref, swap_ref, sums_ref):
    batches = 2
    ext = vb_ref.shape[0] // batches
    toks = ext - HALO
    lanes = vb_ref.shape[1]
    start = s_ref[ME] * toks
    acc = [jnp.zeros((1, lanes), F32) for _ in range(5)]
    products = []
    for m in range(batches):
        own = slice(m * toks, (m + 1) * toks)
        vb = vb_ref[m * ext : (m + 1) * ext]
        dc = dc_ref[own]
        longer = jnp.concatenate([dc, head_ref[m]], axis=0)
        place = start + lax.broadcasted_iota(jnp.int32, dc.shape, 0)
        place_long = start + lax.broadcasted_iota(jnp.int32, longer.shape, 0)
        dvb = jnp.zeros(dc.shape, F32)
        for k in range(4):
            masked = jnp.where(conv_mask(place_long, s_ref[m], k), longer, 0.0)
            dvb = dvb + vec_ref[k : k + 1] * rolled(masked, -k)[:toks]
            prior = rolled(vb, k)[HALO:]
            acc[k] += jnp.sum(jnp.where(conv_mask(place, s_ref[m], k), dc * prior, 0.0), axis=0, keepdims=True)
        acc[4] += jnp.sum(dc, axis=0, keepdims=True)
        dvb16 = dvb.astype(BF16)
        dvb_ref[own] = dvb16
        products.append(dvb16.astype(F32) * vb[HALO:] + dyb_ref[own].astype(F32) * yb_ref[own])
    sums_ref[...] = jnp.zeros_like(sums_ref)
    for k in range(5):
        sums_ref[k : k + 1] = acc[k]
    side = inner_rows(jnp.concatenate(products, axis=0))
    width = keep_ref.shape[2]
    total = batches * toks
    for r, mine, other in chunk_places(s_ref):
        for ref, block in ((swap_ref, other), (keep_ref, mine)):
            here = lane_block(block, width)
            got = mm(dyb_ref[...], w_ref[:lanes, here]) + mm(dvb_ref[...], w_ref[lanes : 2 * lanes, here])
            ref[r, :total] = got.astype(BF16)
            ref[r, total:] = side


def dp_pairs(along_x, by):
    pairs = []
    for y in range(SIDE):
        for x in range(SIDE):
            there = (y * SIDE + (x + by) % SIDE) if along_x else ((y + by) % SIDE * SIDE + x)
            pairs.append((y * SIDE + x, there))
    return pairs


def send(value, along_x, by):
    return lax.ppermute(value, "dp", dp_pairs(along_x, by))


def send_z(value, by):
    return lax.ppermute(value, "mp", [(z * 2 + c, (z + by) % SIDE * 2 + c) for z in range(SIDE) for c in range(2)])


def swap_cores(value):
    return lax.ppermute(value, "mp", [(i, i ^ 1) for i in range(2 * SIDE)])


def relay(value):
    pairs = [(z * 2 + c, (z + (1, -1)[c]) % SIDE * 2 + c) for z in range(SIDE) for c in range(2)]
    return lax.ppermute(value, "mp", pairs)


def gather_mp(value, core):
    low, high = send_z(value, 1), send_z(value, -1)
    three = jnp.stack([value, low, high])
    far = relay(jnp.where(core == 0, low, high))
    return three, far, swap_cores(three), swap_cores(far)


def reduce_mp(keep, swap, core):
    both = keep.astype(F32) + swap_cores(swap).astype(F32)
    passed = relay(both[2].astype(BF16)).astype(F32)
    low = send_z((both[1] + jnp.where(core == 0, passed, 0.0)).astype(BF16), 1)
    high = send_z((both[3] + jnp.where(core == 1, passed, 0.0)).astype(BF16), -1)
    return both[0], low, high


def exchange_z(chunks):
    lines = [[z * 2 + c for z in range(SIDE)] for c in range(2)]
    return lax.all_to_all(chunks, "mp", 0, 0, axis_index_groups=lines, tiled=True)


def exchange(chunks, axis):
    return lax.all_to_all(chunks, axis, 0, 0, tiled=True)


def to_all(value, axis):
    return exchange(jnp.broadcast_to(value[None], (lax.axis_size(axis),) + value.shape), axis)


def inner_column(rows):
    flat = rows.T
    return flat[:, 0:1] + flat[:, 1:2]


def dn2_sum_kernel(got_ref, rho_ref, dn2_ref, inner_ref, many_ref):
    toks = dn2_ref.shape[0]
    total = got_ref[0].astype(F32)
    for j in range(1, got_ref.shape[0]):
        total = total + got_ref[j].astype(F32)
    dn2_ref[...] = total[:toks]
    inner_ref[...] = inner_column(total[toks:]) / rho_ref[...]
    low = total[:toks].astype(BF16)
    for j in range(many_ref.shape[0]):
        many_ref[j] = low


def finish_kernel(both_ref, low_ref, high_ref, x_ref, cot_ref, x2_ref, dn2_ref, rho1_ref, rho2_ref, inner2_ref,
                  gains_ref, conv_ref, gate_ref, grad_ref, pack_ref, *, batches, full):
    total, width = x_ref.shape
    toks = total // batches
    ext = rho1_ref.shape[0] // batches
    got = both_ref[...] + low_ref[...].astype(F32) + high_ref[...].astype(F32)
    dn1, dn2, x2 = got[:total], dn2_ref[...], x2_ref[...]
    x = x_ref[...].astype(F32)
    rho1 = jnp.concatenate([rho1_ref[m * ext + HALO : (m + 1) * ext] for m in range(batches)], axis=0)
    rho2 = rho2_ref[...]
    inner1 = inner_column(got[total:]) / rho1
    gx2 = (cot_ref[...].astype(F32) + rho2 * gains_ref[1:2] * dn2
           - x2 * (rho2 * rho2 * rho2 / full * inner2_ref[...]))
    grad_ref[...] = gx2 + rho1 * gains_ref[0:1] * dn1 - x * (rho1 * rho1 * rho1 / full * inner1)
    gain_grads = (jnp.sum(dn1 * x * rho1, axis=0, keepdims=True), jnp.sum(dn2 * x2 * rho2, axis=0, keepdims=True))
    pack_ref[...] = jnp.zeros_like(pack_ref)
    deep = pack_ref.shape[0]
    sums = jnp.concatenate([conv_ref[:5], gate_ref[:3]], axis=0)
    size = sums.shape[1] // 2
    for i in range(deep):
        few = size // deep
        for j in range(2):
            at = j * size + i * few
            pack_ref[i, 8 * j : 8 * j + 8, :few] = sums[:, at : at + few]
        for k, row in enumerate(gain_grads):
            pack_ref[i, 16 + k : 17 + k, : width // deep] = row[:, i * (width // deep) : (i + 1) * (width // deep)]


def small_out_kernel(got_ref, taps_ref, shift_ref, rate_ref, input_ref, decay_ref, one_ref, two_ref):
    total = got_ref[0]
    for i in range(1, got_ref.shape[0]):
        total = total + got_ref[i]
    few = shift_ref.shape[1]
    for j in range(2):
        for k in range(4):
            taps_ref[k, j : j + 1, :] = total[8 * j + k : 8 * j + k + 1, :few]
        for k, ref in enumerate((shift_ref, rate_ref, input_ref, decay_ref)):
            ref[j : j + 1, :] = total[8 * j + 4 + k : 8 * j + 5 + k, :few]
    one_ref[...] = total[16:17, : one_ref.shape[1]]
    two_ref[...] = total[17:18, : two_ref.shape[1]]


def late_kernel(dvb_ref, n1_ref, c_ref, dza_ref, dzx_ref, out_ref):
    deep, _, rows = out_ref.shape
    lanes = dvb_ref.shape[1]
    size = lanes // 2
    few = size // deep
    for i in range(0, deep, SIDE):
        got = mm_tn(dvb_ref[...], n1_ref[:, i * rows : (i + SIDE) * rows]).astype(BF16)
        for d in range(SIDE):
            out_ref[i + d, :lanes] = got[:, d * rows : (d + 1) * rows]
    out_ref[:, lanes:] = jnp.zeros((deep, out_ref.shape[1] - lanes, rows), BF16)
    for kind, ref in enumerate((dza_ref, dzx_ref)):
        both = mm_tn(c_ref[...], ref[...])
        for j in range(2):
            k = 2 * kind + j
            block = both[j * size : (j + 1) * size, j * size : (j + 1) * size].astype(BF16)
            for i in range(deep):
                part = block[i * few : (i + 1) * few]
                out_ref[i, lanes + 16 * k : lanes + 16 * k + few] = part[:, :rows]
                at = lanes + 64 + 16 * (k // 2)
                here = slice(64 * (k % 2), 64 * (k % 2) + size - rows)
                out_ref[i, at : at + few, here] = part[:, rows:]


def late_out_kernel(got_ref, value_ref, rate_ref, input_ref):
    lanes, rows = value_ref.shape
    few, _, size = rate_ref.shape
    total = got_ref[0].astype(F32)
    for i in range(1, got_ref.shape[0]):
        total = total + got_ref[i].astype(F32)
    value_ref[...] = total[:lanes]
    for kind, ref in enumerate((rate_ref, input_ref)):
        for j in range(2):
            k = 2 * kind + j
            at = lanes + 16 * k
            ref[:, j, :rows] = total[at : at + few]
            at = lanes + 64 + 16 * (k // 2)
            ref[:, j, rows:] = total[at : at + few, 64 * (k % 2) : 64 * (k % 2) + size - rows]


def early_out_kernel(got_ref, out_ref, branch_ref):
    lanes = out_ref.shape[0]
    out_ref[...] = got_ref[:lanes].astype(F32)
    branch_ref[...] = got_ref[lanes:].astype(F32)


def beside(at):
    return at + 1 - 2 * (at % 2)


def across(at):
    return SIDE - 1 - at


def send_to(value, along_x, partner):
    pairs = []
    for y in range(SIDE):
        for x in range(SIDE):
            there = (y * SIDE + partner(x)) if along_x else (partner(y) * SIDE + x)
            pairs.append((y * SIDE + x, there))
    return lax.ppermute(value, "dp", pairs)


def at_of(s_ref, along_x):
    return s_ref[COL_X if along_x else ROW_Y]


def partners_of(one_set):
    return (beside, across) if one_set[3] is beside else (across, beside)


def whole_spec(dims):
    return pl.BlockSpec(dims, lambda i: (0,) * len(dims))


def half_spec(units, wide, index):
    return pl.BlockSpec((units, wide), lambda i: (0, index))


def call_whole(name, kernel, outs, args, specs=None, scratch=(), ties=()):
    ins = [SCALARS if v.dtype == jnp.int32 else whole_spec(v.shape) for v in args]
    for k, spec in (specs or {}).items():
        ins[k] = spec
    return call(kernel, outs, ins, args, grid=(1,), out_specs=[whole_spec(o.shape) for o in outs], scratch=scratch,
                name=name, ties=ties)


def halving_one(name, scalars, group, wide, ties=()):
    operands, sets = group

    def kernel(s_ref, *refs):
        ins, outs = refs[: len(operands)], refs[len(operands) :]
        for one_set, out_ref in zip(sets, outs):
            first, second = partners_of(one_set)
            there = first(at_of(s_ref, one_set[2]))
            out_ref[:, :wide] = one_set[0](ins, there).astype(BF16)
            out_ref[:, wide:] = one_set[0](ins, second(there)).astype(BF16)

    outs = [shape((t[1], 2 * wide), BF16) for t in sets]
    sent = call_whole(name, kernel, outs, (scalars, *operands), ties=ties)
    return sent, [send_to(v, t[2], partners_of(t)[0]) for v, t in zip(sent, sets)]


def halving_two(name, scalars, group, wide, got, ties=()):
    operands, sets = group

    def kernel(s_ref, *refs):
        ins, got, outs = refs[: len(operands)], refs[len(operands) : -len(sets)], refs[-len(sets) :]
        for one_set, got_ref, out_ref in zip(sets, got, outs):
            there = partners_of(one_set)[1](at_of(s_ref, one_set[2]))
            out_ref[...] = (one_set[0](ins, there) + got_ref[...].astype(F32)).astype(BF16)

    outs = [shape((t[1], wide), BF16) for t in sets]
    specs = {1 + len(operands) + k: half_spec(t[1], wide, 1) for k, t in enumerate(sets)}
    sent = call_whole(name, kernel, outs, (scalars, *operands, *got), specs, ties=ties)
    return sent, [send_to(v, t[2], partners_of(t)[1]) for v, t in zip(sent, sets)]


def halving_three(name, scalars, group, wide, got_one, got_two, ties=()):
    size = wide // SIDE
    operands, sets = group
    tall = [sum(t[1] for t in sets if t[2] == along_x) for along_x in (False, True)]
    count = len(operands)

    def kernel(s_ref, *refs):
        ins, ones, twos = refs[:count], refs[count : count + len(sets)], refs[count + len(sets) : -2 * SIDE - 1]
        outs, held = refs[-2 * SIDE - 1 : -1], refs[-1]
        start = [0, 0]
        for (chunk, units, along_x, _), one, two in zip(sets, ones, twos):
            held[:units] = chunk(ins, at_of(s_ref, along_x)) + one[...].astype(F32) + two[...].astype(F32)
            here = slice(start[along_x], start[along_x] + units)
            start[along_x] += units
            for d in range(SIDE):
                ref = outs[SIDE * along_x + d]
                at = (at_of(s_ref, not along_x) + d) % SIDE
                ref[here] = held[:units, lane_block(at, size)].astype(ref.dtype)

    outs = [shape((tall[k], size), BF16 if d else F32) for k in range(2) for d in range(SIDE)]
    specs = {1 + count + k: half_spec(t[1], wide, 0) for k, t in enumerate(sets)}
    parts = call_whole(name, kernel, outs, (scalars, *operands, *got_one, *got_two), specs,
                       [pltpu.VMEM((max(t[1] for t in sets), wide), F32)], ties)
    return [parts[SIDE * k + d] if d == 0 else send(parts[SIDE * k + d], not k, d) for k in range(2) for d in range(SIDE)]


def block_diagonal(blocks):
    count, size = blocks.shape[0], blocks.shape[1]
    rows = [jnp.pad(blocks[j], ((0, 0), (j * size, (count - 1 - j) * size))) for j in range(count)]
    return jnp.concatenate(rows, axis=0)


def body(inputs, cotangent, row_split, first_gain, branch_weight, value_weight, conv_weight, conv_bias,
         rate_blocks, input_blocks, rate_bias, input_bias, decay_param, out_weight, second_gain,
         gate_weight, up_weight, down_weight):
    batches, toks, width = inputs.shape
    parts = lax.axis_size("mp")
    deep = lax.axis_size("dp")
    full = width * parts
    blocks, size = rate_blocks.shape[0], rate_blocks.shape[1]
    lanes = blocks * size
    rows = branch_weight.shape[0]
    units = gate_weight.shape[1]
    total = batches * toks
    ext = toks + HALO
    me = lax.axis_index("dp")
    at_mp = lax.axis_index("mp")
    core = at_mp % 2
    scalars = jnp.concatenate(
        [row_split, jnp.stack([me, me // SIDE, me % SIDE, at_mp // 2, core, jnp.zeros_like(me)])]).astype(jnp.int32)

    w_rec = lax.all_gather(jnp.concatenate([branch_weight.T, value_weight.T, out_weight], axis=0), "dp")
    w_ffn = lax.all_gather(jnp.stack([gate_weight, up_weight, down_weight.T]), "dp")

    decay = decay_param.reshape(1, lanes).astype(F32)
    vectors = jnp.concatenate(
        [conv_weight.reshape(4, lanes).astype(F32), conv_bias.reshape(1, lanes).astype(F32),
         rate_bias.reshape(1, lanes).astype(F32), input_bias.reshape(1, lanes).astype(F32),
         8.0 * jax.nn.softplus(decay), 8.0 * jax.nn.sigmoid(decay), jnp.zeros((7, lanes), F32)], axis=0)
    rate_mat = block_diagonal(rate_blocks)
    input_mat = block_diagonal(input_blocks)

    pairs = [(i, i + 1) for i in range(deep - 1)]
    before = lax.ppermute(inputs[:, toks - HALO :], "dp", pairs)
    gains = jnp.concatenate([first_gain[None], second_gain[None], jnp.zeros((HALO - 2, width), BF16)], axis=0)
    payload = jnp.concatenate([jnp.concatenate([before, inputs], axis=1).reshape(batches * ext, width), gains], axis=0)
    x_parts = gather_mp(payload, core)
    n1, n1_own, rho1, gain_rows = call(
        norm_one_kernel,
        [shape((batches * ext, full), BF16), shape((total, full), BF16), shape((batches * ext, 1)), shape((HALO, full))],
        [SCALARS] + [WHOLE] * 4, (scalars, *x_parts),
        scratch=[pltpu.VMEM((batches * ext, full), BF16)], name="norm_one")
    cot_parts = gather_mp(cotangent.reshape(total, width), core)

    grown = shape((total, lanes))

    def full_spec(dims):
        return pl.BlockSpec(dims, lambda i: (0,) * len(dims))

    w_rec, yb, vb, c, rate, gate, a, prod, state, last = call(
        rec_fwd_kernel,
        [shape((3 * lanes, full), BF16), grown, shape((batches * ext, lanes)), shape((total, lanes), BF16)]
        + [grown] * 5 + [shape((8, lanes))],
        [SCALARS] + [WHOLE] * 5,
        (scalars, n1, w_rec, vectors, rate_mat, input_mat), name="rec_fwd", ties=cot_parts)
    ends = to_all(last, "dp")
    chunk = shape((SIDE, total, width), BF16)
    chunk_long = shape((SIDE, total + HALO, width), BF16)
    def with_weights(kernel, outs, args, w_at, blocks_at, name, ties=()):
        ins = [SCALARS if a.dtype == jnp.int32 else full_spec(a.shape) for a in args]
        ins[w_at] = pl.BlockSpec((blocks_at[1] * lanes, full), lambda i: (blocks_at[0], 0))
        return call(kernel, outs, ins, args, grid=(1,), out_specs=[full_spec(o.shape) for o in outs],
                    name=name, ties=ties)

    h, carry, o, keep, swap = with_weights(
        rec_out_kernel, [grown, shape((8, lanes)), shape((total, lanes), BF16), chunk, chunk],
        (scalars, ends, prod, state, yb, w_rec), 5, (2, 1), "rec_out")
    x_own = inputs.reshape(total, width).astype(F32)
    both, low, high = reduce_mp(keep, swap, core)
    x2 = x_own + (both + low.astype(F32) + high.astype(F32))
    x2_parts = gather_mp(x2.astype(BF16), core)

    steps = 3
    cols = units // steps
    n2, x2_full, rho2, cot_full, hid, dgt, dup, part_o, keep, swap = call(
        ffn_kernel,
        [shape((total, full), BF16)] * 2 + [shape((total, 1)), shape((total, full), BF16)]
        + [shape((total, units), BF16)] * 3
        + [shape((total, full), BF16), chunk_long, chunk_long],
        [SCALARS] + [full_spec(v.shape) for v in x2_parts + cot_parts] + [full_spec(gain_rows.shape),
         pl.BlockSpec((deep, 3, rows, cols), lambda g: (0, 0, 0, g))],
        (scalars, *x2_parts, *cot_parts, gain_rows, w_ffn),
        grid=(steps,),
        out_specs=[full_spec((total, full))] * 2 + [full_spec((total, 1)), full_spec((total, full))]
        + [pl.BlockSpec((total, cols), lambda g: (0, g))] * 3
        + [full_spec((total, full)), full_spec(chunk_long.shape), full_spec(chunk_long.shape)],
        scratch=[pltpu.VMEM((total, full), F32), pltpu.VMEM((total, full), F32), pltpu.VMEM((total, cols), F32)],
        name="ffn")

    def row_lanes(ref, at):
        return ref[:, lane_block(at, SIDE * rows)]

    def column_lanes(ref, at):
        return jnp.concatenate([ref[:, lane_block(y * SIDE + at, rows)] for y in range(SIDE)], axis=1)

    mid, low = units // 2, units // 4

    def ffn_set(along_x, second):
        lanes_of = column_lanes if along_x else row_lanes
        main = slice(second * mid, (second + 1) * mid)
        part = slice((2 * along_x + second) * low, (2 * along_x + second + 1) * low)

        def chunk(refs, at):
            n2_ref, cot_ref, hid_ref = refs[0], refs[1], refs[4]
            grad_ref = refs[3] if along_x else refs[2]
            return jnp.concatenate(
                [mm_tn(grad_ref[:, main], lanes_of(n2_ref, at)), mm_tn(hid_ref[:, part], lanes_of(cot_ref, at))], axis=0)

        return chunk, mid + low, along_x, across if second else beside

    wide = SIDE * rows
    ffn_group = ((n2, cot_full, dgt, dup, hid),
                 [ffn_set(along_x, second) for along_x in (False, True) for second in (False, True)])
    dn2_parts = (keep.astype(F32) + swap_cores(swap).astype(F32)).astype(BF16)
    ffn_one, ffn_got_one = halving_one("ffn_grad_one", scalars, ffn_group, wide, (dn2_parts,))
    layer_part = lax.psum_scatter(part_o, "mp", scatter_dimension=1, tiled=True)
    got = exchange_z(dn2_parts)
    dn2, inner2, dn2_many = call(
        dn2_sum_kernel, [shape((total, width)), shape((total, 1)), shape((SIDE, total, width), BF16)], [WHOLE] * 2,
        (got, rho2), name="dn2_sum", ties=(ffn_one[0],))
    dn2_line = exchange_z(dn2_many)

    gr, dyb, adj, adj_prod, first = with_weights(
        rec_bwd_kernel,
        [shape((total, full), BF16), shape((total, lanes), BF16), grown, grown, shape((deep, 8, lanes))],
        (scalars, dn2_line, swap_cores(dn2_line), x2_full, cot_full, gain_rows, rho2, inner2, w_rec, yb, h, a, prod),
        8, (2, 1), "rec_bwd")

    starts = exchange(first, "dp")

    def early_kernel(o_ref, gr_ref, dyb_ref, n1_ref, out_ref):
        for k, (left, right) in enumerate(((o_ref, gr_ref), (dyb_ref, n1_ref))):
            units_at = slice(k * lanes, (k + 1) * lanes)
            for i in range(0, deep, SIDE):
                got = mm_tn(left[...], right[:, i * rows : (i + SIDE) * rows]).astype(BF16)
                for d in range(SIDE):
                    out_ref[i + d, units_at] = got[:, d * rows : (d + 1) * rows]

    early = call(early_kernel, [shape((deep, 2 * lanes, rows), BF16)], [WHOLE] * 4, (o, gr, dyb, n1_own),
                 name="early_grad", ties=tuple(ffn_got_one))[0]
    ffn_two, ffn_got_two = halving_two("ffn_grad_two", scalars, ffn_group, wide, ffn_got_one, (early,))
    early = lax.psum_scatter(early.reshape(-1, rows), "dp", scatter_dimension=0, tiled=True)

    dza, dzx, dc, head, sums_gate = call(
        gate_bwd_kernel,
        [shape((total, lanes), BF16)] * 2 + [grown, shape((batches, 8, lanes)), shape((8, lanes))],
        [SCALARS] + [WHOLE] * 12,
        (scalars, starts, adj, adj_prod, a, h, carry, c, rate, gate, vectors, rate_mat, input_mat),
        name="gate_bwd", ties=(ffn_two[0],))
    following = lax.ppermute(head, "dp", [(i + 1, i) for i in range(deep - 1)])
    dvb, keep, swap, sums_conv = with_weights(
        conv_bwd_kernel,
        [shape((total, lanes), BF16), chunk_long, chunk_long, shape((8, lanes))],
        (scalars, dc, following, vb, yb, dyb, vectors, w_rec), 7, (0, 2), "conv_bwd")
    late = call(late_kernel, [shape((deep, lanes + 96, rows), BF16)], [WHOLE] * 5, (dvb, n1_own, c, dza, dzx),
                name="late_grad", ties=tuple(ffn_got_two))[0]
    keep, late = lax.optimization_barrier((keep, late))
    late_got = exchange(late, "dp")
    both, below, above = reduce_mp(keep, swap, core)
    grad_sums = halving_three("ffn_grad_three", scalars, ffn_group, wide, ffn_got_one, ffn_got_two, (late,))
    layer_out = (x2 + layer_part.astype(F32)).astype(BF16)
    small_gains = jnp.stack([first_gain, second_gain]).astype(F32)
    input_grad, pack = call(
        functools.partial(finish_kernel, batches=batches, full=full),
        [shape((total, width)), shape((deep, 24, rows))], [WHOLE] * 13,
        (both, below, above, inputs.reshape(total, width), cotangent.reshape(total, width), x2, dn2, rho1, rho2, inner2,
         small_gains, sums_conv, sums_gate), name="finish")
    few = size // deep
    pair = shape((blocks, few))
    pack, late_got = lax.optimization_barrier((pack, late_got))
    value_grad, rate_g, input_g = call(
        late_out_kernel, [shape((lanes, rows))] + [shape((few, blocks, size))] * 2, [WHOLE], (late_got,),
        name="late_out")
    taps, shift, rate_b, input_b, decay_g, gain_a, gain_b = call(
        small_out_kernel, [shape((4, blocks, few)), pair, pair, pair, pair] + [shape((1, width // deep))] * 2, [WHOLE],
        (exchange(pack, "dp"),), name="small_out")
    out_grad, branch_grad = call(early_out_kernel, [shape((lanes, rows))] * 2, [WHOLE], (early,), name="early_out")

    def ffn_out_kernel(*refs):
        outs = refs[2 * SIDE :]
        for k in range(2):
            for second in range(2):
                at = second * (mid + low)
                sums = [sum(ref[there].astype(F32) for ref in refs[SIDE * k : SIDE * k + SIDE])
                        for there in (slice(at, at + mid), slice(at + mid, at + mid + low))]
                outs[k][:, second * mid : (second + 1) * mid] = sums[0].T
                outs[2][(2 * k + second) * low : (2 * k + second + 1) * low] = sums[1]

    gate_grad, up_grad, down = call(
        ffn_out_kernel, [shape((rows, units))] * 2 + [shape((units, rows))], [WHOLE] * (2 * SIDE),
        grad_sums, name="ffn_out", ties=(pack, value_grad, out_grad))

    return (
        layer_out.reshape(batches, toks, width), input_grad.reshape(batches, toks, width),
        gain_a.reshape(-1), branch_grad.T, value_grad.T, taps, shift, rate_g.transpose(1, 0, 2),
        input_g.transpose(1, 0, 2), rate_b, input_b, decay_g,
        out_grad, gain_b.reshape(-1), gate_grad, up_grad, down,
    )


def solution(mesh):
    placed = (
        P(None, "dp", "mp"), P(None, "dp", "mp"), P(), P("mp"), P("dp", "mp"), P("dp", "mp"),
        P(None, "mp", None), P("mp", None), P("mp", None, None), P("mp", None, None), P("mp", None),
        P("mp", None), P("mp", None), P("mp", "dp"), P("mp"), P("dp", "mp"), P("dp", "mp"), P("mp", "dp"),
    )
    given = (
        P(None, "dp", "mp"), P(None, "dp", "mp"), P(("mp", "dp")), P("dp", "mp"), P("dp", "mp"),
        P(None, "mp", "dp"), P("mp", "dp"), P("mp", "dp", None), P("mp", "dp", None), P("mp", "dp"),
        P("mp", "dp"), P("mp", "dp"), P("mp", "dp"), P(("mp", "dp")), P("dp", "mp"), P("dp", "mp"), P("mp", "dp"),
    )
    return jax.shard_map(body, mesh=mesh, in_specs=placed, out_specs=given, check_vma=False)
```

```python
import functools
import math

import jax
import jax.numpy as jnp
from jax import lax
from jax.experimental import pallas as pl
from jax.experimental.pallas import tpu as pltpu
from jax.sharding import PartitionSpec as P

EPS = 1e-06
F32 = jnp.float32
BF16 = jnp.bfloat16
NT = (((1,), (1,)), ((), ()))
TN = (((0,), (0,)), ((), ()))
HALO = 16
SIDE = 4
VMEM_BYTES = 56 * 1024 * 1024
FLOPS_PER_US = 1.15e9
COST_US = {
    "norm_one": 3.5, "rec_fwd": 8.4, "rec_out": 3.7, "ffn": 11.0, "ffn_grad_one": 5.0, "ffn_grad_two": 0.3,
    "ffn_grad_three": 6.3, "ffn_out": 3.0, "norm_two": 4.0, "dn2_sum": 0.3, "rec_bwd": 0.3, "early_grad": 0.3,
    "early_out": 1.7,
    "gate_bwd": 3.9, "conv_bwd": 5.7, "late_grad": 0.3, "finish": 2.8, "small_out": 1.5, "late_out": 2.5,
}
GELU_K = math.sqrt(2.0 / math.pi)


def mm(a, b):
    return jnp.dot(a, b, preferred_element_type=F32)


def mm_nt(a, b):
    return lax.dot_general(a, b, NT, preferred_element_type=F32)


def mm_tn(a, b):
    return lax.dot_general(a, b, TN, preferred_element_type=F32)


def gelu_pair(x):
    t = jnp.tanh(GELU_K * (x + 0.044715 * (x * x * x)))
    half = 0.5 * (1.0 + t)
    slope = half + 0.5 * x * (1.0 - t * t) * (GELU_K * (1.0 + 0.134145 * (x * x)))
    return x * half, slope


def neg_expm1(x):
    near = jnp.maximum(x, -0.5)
    series = 1.0 / 40320.0 + near * (1.0 / 362880.0)
    for denom in (5040.0, 720.0, 120.0, 24.0, 6.0, 2.0, 1.0):
        series = 1.0 / denom + near * series
    return jnp.where(x > -0.5, -near * series, 1.0 - jnp.exp(x))


def rolled(x, by):
    return x if by == 0 else jnp.roll(x, by, axis=0)


def shift_down(x, step, fill):
    rows = lax.broadcasted_iota(jnp.int32, x.shape, 0)
    return jnp.where(rows < step, fill, jnp.roll(x, step, axis=0))


def shift_up(x, step, fill):
    count = x.shape[0]
    rows = lax.broadcasted_iota(jnp.int32, x.shape, 0)
    return jnp.where(rows >= count - step, fill, jnp.roll(x, -step, axis=0))


def scan_down(a, u):
    step = 1
    while step < a.shape[0]:
        u = u + a * shift_down(u, step, 0.0)
        a = a * shift_down(a, step, 1.0)
        step *= 2
    return a, u


def scan_up(a, u):
    step = 1
    while step < a.shape[0]:
        u = u + a * shift_up(u, step, 0.0)
        a = a * shift_up(a, step, 1.0)
        step *= 2
    return a, u


def conv_mask(place, split_at, back):
    behind = place - back
    return ((behind >= split_at) == (place >= split_at)) & (behind >= 0)


def call(kernel, outs, ins, args, grid=None, out_specs=None, scratch=(), name=None, ties=()):
    kwargs = {}
    if ties:
        count, inner = len(args), kernel

        def kernel(*refs):
            inner(*refs[:count], *refs[count + len(ties) :])

        ins = list(ins) + [pl.BlockSpec(memory_space=pl.ANY)] * len(ties)
        args = tuple(args) + tuple(ties)
    if grid is not None:
        kwargs["grid"] = grid
    return pl.pallas_call(
        kernel,
        out_shape=outs,
        in_specs=ins,
        out_specs=out_specs if out_specs is not None else [WHOLE] * len(outs),
        scratch_shapes=list(scratch),
        compiler_params=pltpu.CompilerParams(vmem_limit_bytes=VMEM_BYTES),
        cost_estimate=pl.CostEstimate(flops=int(COST_US[name] * FLOPS_PER_US), bytes_accessed=0, transcendentals=0),
        name=name,
        **kwargs,
    )(*args)


WHOLE = pl.BlockSpec(memory_space=pltpu.VMEM)
SCALARS = pl.BlockSpec(memory_space=pltpu.SMEM)
ME, ROW_Y, COL_X, DEEP_Z, CORE = 2, 3, 4, 5, 6
NEAR = (0, -1, 1)


def shape(dims, dtype=F32):
    return jax.ShapeDtypeStruct(dims, dtype)


def lane_block(index, width):
    return pl.ds(pl.multiple_of(index * width, width), width)


def lay_parts(s_ref, three, far, three_other, far_other, put):
    z, core = s_ref[DEEP_Z], s_ref[CORE]
    for held, held_far, which in ((three, far, core), (three_other, far_other, 1 - core)):
        for k, dz in enumerate(NEAR):
            put((z + dz + SIDE) % SIDE * 2 + which, held[k])
        put((z + 2) % SIDE * 2 + which, held_far[...])


def norm_one_kernel(s_ref, three, far, three_other, far_other, n1_ref, own_ref, rho_ref, gain_ref, x_ref):
    rows = three.shape[1] - HALO
    width = three.shape[2]
    full = x_ref.shape[1]

    def put(block, value):
        here = lane_block(block, width)
        x_ref[:, here] = value[:rows]
        gain_ref[:, here] = value[rows:].astype(F32)

    lay_parts(s_ref, three, far, three_other, far_other, put)
    total = jnp.zeros((rows, 1), F32)
    for j in range(full // width):
        xj = x_ref[:, j * width : (j + 1) * width].astype(F32)
        total = total + jnp.sum(xj * xj, axis=1, keepdims=True)
    rho = lax.rsqrt(total / full + EPS)
    rho_ref[...] = rho
    batches = own_ref.shape[0] // (rows // 2 - HALO)
    ext = rows // batches
    toks = ext - HALO
    for j in range(full // width):
        here = slice(j * width, (j + 1) * width)
        n1 = (x_ref[:, here].astype(F32) * rho * gain_ref[0:1, here]).astype(BF16)
        n1_ref[:, here] = n1
        for m in range(batches):
            own_ref[m * toks : (m + 1) * toks, here] = n1[m * ext + HALO : (m + 1) * ext]


def rec_fwd_kernel(s_ref, n1_ref, shards_ref, vec_ref, wr_ref, wi_ref,
                   w_ref, yb_ref, vb_ref, c_ref, r_ref, i_ref, a_ref, pr_ref, st_ref, last_ref):
    batches = 2
    ext = n1_ref.shape[0] // batches
    toks = ext - HALO
    lanes = vec_ref.shape[1]
    piece = shards_ref.shape[2]
    for i in range(shards_ref.shape[0]):
        w_ref[:, i * piece : (i + 1) * piece] = shards_ref[i]
    start = s_ref[ME] * toks
    vb_ref[...] = mm_nt(n1_ref[...], w_ref[lanes : 2 * lanes])
    last_ref[...] = jnp.zeros_like(last_ref)
    for m in range(batches):
        own = slice(m * toks, (m + 1) * toks)
        yb_ref[own] = mm_nt(n1_ref[m * ext + HALO : (m + 1) * ext], w_ref[:lanes])
        vb = vb_ref[m * ext : (m + 1) * ext]
        place = start + lax.broadcasted_iota(jnp.int32, (toks, lanes), 0)
        split_at = s_ref[m]
        conv = jnp.zeros((toks, lanes), F32) + vec_ref[4:5]
        for k in range(4):
            term = vec_ref[k : k + 1] * rolled(vb, k)[HALO:]
            conv = conv + jnp.where(conv_mask(place, split_at, k), term, 0.0)
        c16 = conv.astype(BF16)
        c = c16.astype(F32)
        rate = jax.nn.sigmoid(mm(c16, wr_ref[...]) + vec_ref[5:6])
        gate = jax.nn.sigmoid(mm(c16, wi_ref[...]) + vec_ref[6:7])
        la = -vec_ref[7:8] * rate
        keep = (place != split_at).astype(F32)
        a = keep * jnp.exp(la)
        u = (keep * jnp.sqrt(neg_expm1(2.0 * la)) + (1.0 - keep)) * gate * c
        c_ref[own] = c16
        r_ref[own] = rate
        i_ref[own] = gate
        a_ref[own] = a
        prod, state = scan_down(a, u)
        pr_ref[own] = prod
        st_ref[own] = state
        last_ref[2 * m : 2 * m + 1] = prod[toks - 1 :]
        last_ref[2 * m + 1 : 2 * m + 2] = state[toks - 1 :]


def carry_of(s_ref, all_ref, m, backward):
    me = s_ref[ME]
    count = all_ref.shape[0]
    carry = jnp.zeros((1, all_ref.shape[2]), F32)
    for q in range(count - 1, 0, -1) if backward else range(count - 1):
        longer = all_ref[q, 2 * m : 2 * m + 1] * carry + all_ref[q, 2 * m + 1 : 2 * m + 2]
        carry = jnp.where((q > me) if backward else (q < me), longer, carry)
    return carry


def chunk_places(s_ref):
    z, core = s_ref[DEEP_Z], s_ref[CORE]
    for r in range(SIDE):
        yield r, (z + r) % SIDE * 2 + core, (z + r) % SIDE * 2 + 1 - core


def rec_out_kernel(s_ref, all_ref, pr_ref, st_ref, yb_ref, w_ref,
                   h_ref, carry_ref, o_ref, keep_ref, swap_ref):
    batches = 2
    toks = pr_ref.shape[0] // batches
    carry_ref[...] = jnp.zeros_like(carry_ref)
    for m in range(batches):
        own = slice(m * toks, (m + 1) * toks)
        carry = carry_of(s_ref, all_ref, m, False)
        carry_ref[m : m + 1] = carry
        h = st_ref[own] + pr_ref[own] * carry
        h_ref[own] = h
        o_ref[own] = (h * gelu_pair(yb_ref[own])[0]).astype(BF16)
    width = keep_ref.shape[2]
    for r, mine, other in chunk_places(s_ref):
        swap_ref[r] = mm(o_ref[...], w_ref[:, lane_block(other, width)]).astype(BF16)
        keep_ref[r] = mm(o_ref[...], w_ref[:, lane_block(mine, width)]).astype(BF16)


def inner_rows(products):
    ones = jnp.ones((HALO, products.shape[1]), F32)
    sums = lax.dot_general(ones, products, NT, precision=lax.Precision.HIGHEST, preferred_element_type=F32)
    high = sums.astype(BF16)
    low = (sums - high.astype(F32)).astype(BF16)
    rows = lax.broadcasted_iota(jnp.int32, sums.shape, 0)
    return jnp.where(rows == 0, high.astype(F32), jnp.where(rows == 1, low.astype(F32), 0.0)).astype(BF16)


def norm_two_kernel(s_ref, three, far, three_other, far_other, c3_ref, cf_ref, c3o_ref, cfo_ref, gain_ref,
                    n2_ref, x2_ref, rho_ref, cotf_ref):
    _, toks, width = three.shape
    full = x2_ref.shape[1]

    def put(block, value):
        x2_ref[:, lane_block(block, width)] = value

    def put_cot(block, value):
        cotf_ref[:, lane_block(block, width)] = value

    lay_parts(s_ref, three, far, three_other, far_other, put)
    lay_parts(s_ref, c3_ref, cf_ref, c3o_ref, cfo_ref, put_cot)
    total = jnp.zeros((toks, 1), F32)
    for j in range(full // width):
        xj = x2_ref[:, j * width : (j + 1) * width].astype(F32)
        total = total + jnp.sum(xj * xj, axis=1, keepdims=True)
    rho = lax.rsqrt(total / full + EPS)
    rho_ref[...] = rho
    for j in range(full // width):
        here = slice(j * width, (j + 1) * width)
        n2_ref[:, here] = (x2_ref[:, here].astype(F32) * rho * gain_ref[1:2, here]).astype(BF16)


def ffn_kernel(s_ref, n2_ref, cotf_ref, w_ref,
               hid_ref, dgt_ref, dup_ref, po_ref, keep_ref, swap_ref,
               acc_o, acc_d, acc_i):
    step = pl.program_id(0)
    deep, _, rows, cols = w_ref.shape
    toks = n2_ref.shape[0]
    width = keep_ref.shape[2]

    @pl.when(step == 0)
    def _():
        acc_o[...] = jnp.zeros_like(acc_o)
        acc_d[...] = jnp.zeros_like(acc_d)
        acc_i[...] = jnp.zeros_like(acc_i)

    wg = w_ref[:, 0].reshape(deep * rows, cols)
    wu = w_ref[:, 1].reshape(deep * rows, cols)
    wd = w_ref[:, 2].reshape(deep * rows, cols)
    gt = mm(n2_ref[...], wg)
    up = mm(n2_ref[...], wu)
    dm = mm(cotf_ref[...], wd)
    act, slope = gelu_pair(gt)
    hid = (act * up).astype(BF16)
    dgt = (slope * up * dm).astype(BF16)
    dup = (act * dm).astype(BF16)
    hid_ref[...] = hid
    dgt_ref[...] = dgt
    dup_ref[...] = dup
    acc_i[...] += dgt.astype(F32) * gt + dup.astype(F32) * up
    acc_o[...] += mm_nt(hid, wd)
    acc_d[...] += mm_nt(dgt, wg) + mm_nt(dup, wu)

    @pl.when(step == pl.num_programs(0) - 1)
    def _():
        side = inner_rows(acc_i[...])
        po_ref[...] = acc_o[...].astype(BF16)
        core = s_ref[CORE]
        for z in range(SIDE):
            for ref, block in ((swap_ref, 2 * z + 1 - core), (keep_ref, 2 * z + core)):
                ref[z, :toks] = acc_d[:, lane_block(block, width)].astype(BF16)
                ref[z, toks:] = side


def rec_bwd_kernel(s_ref, dn2_ref, other_ref, x2_ref, cotf_ref, gain_ref, rho_ref, inner_ref, w_ref,
                   yb_ref, h_ref, a_ref, pr_ref,
                   gr_ref, dyb_ref, la_ref, lp_ref, first_ref):
    width = dn2_ref.shape[2]
    full = x2_ref.shape[1]
    batches = 2
    toks = x2_ref.shape[0] // batches
    rho = rho_ref[...]
    back = rho * rho * rho / full * inner_ref[...]

    core = s_ref[CORE]
    for z in range(SIDE):
        for ref, block in ((dn2_ref, 2 * z + core), (other_ref, 2 * z + 1 - core)):
            here = lane_block(block, width)
            gx2 = (cotf_ref[:, here].astype(F32) + rho * gain_ref[1:2, here] * ref[z].astype(F32)
                   - x2_ref[:, here].astype(F32) * back)
            gr_ref[:, here] = gx2.astype(BF16)
    do = mm_nt(gr_ref[...], w_ref[...])
    ends = []
    for m in range(batches):
        own = slice(m * toks, (m + 1) * toks)
        act, slope = gelu_pair(yb_ref[own])
        dom = do[own]
        dyb_ref[own] = (slope * h_ref[own] * dom).astype(BF16)
        a = a_ref[own]
        prod, adj = scan_up(shift_up(a, 1, 1.0), dom * act)
        la_ref[own] = adj
        lp_ref[own] = prod
        ends += [pr_ref[(m + 1) * toks - 1 : (m + 1) * toks], a[0:1] * adj[0:1]]
    ends = jnp.concatenate(ends + [jnp.zeros_like(ends[0])] * (first_ref.shape[1] - len(ends)), axis=0)
    for i in range(first_ref.shape[0]):
        first_ref[i] = ends


def gate_bwd_kernel(s_ref, all_ref, la_ref, lp_ref, a_ref, h_ref, carry_ref, c_ref, r_ref,
                    i_ref, vec_ref, wr_ref, wi_ref, dza_ref, dzx_ref, dc_ref, head_ref, sums_ref):
    batches = 2
    toks = la_ref.shape[0] // batches
    lanes = la_ref.shape[1]
    start = s_ref[ME] * toks
    lam = vec_ref[7:8]
    acc = [jnp.zeros((1, lanes), F32) for _ in range(3)]
    for m in range(batches):
        own = slice(m * toks, (m + 1) * toks)
        q = la_ref[own] + lp_ref[own] * carry_of(s_ref, all_ref, m, True)
        rows = lax.broadcasted_iota(jnp.int32, (toks, lanes), 0)
        keep = (start + rows != s_ref[m]).astype(F32)
        hprev = jnp.where(rows == 0, carry_ref[m : m + 1], jnp.roll(h_ref[own], 1, axis=0))
        rate = r_ref[own]
        gate = i_ref[own]
        c = c_ref[own].astype(F32)
        la = -lam * rate
        root = jnp.sqrt(neg_expm1(2.0 * la))
        decay = jnp.exp(la)
        scaled = keep * root + (1.0 - keep)
        dla = q * hprev * keep * decay - q * keep * gate * c * (decay * decay / root)
        dza = (dla * (-lam) * rate * (1.0 - rate)).astype(BF16)
        dc0 = q * scaled * gate
        dzx = (dc0 * c * (1.0 - gate)).astype(BF16)
        dza_ref[own] = dza
        dzx_ref[own] = dzx
        dc = dc0 + mm_nt(dza, wr_ref[...]) + mm_nt(dzx, wi_ref[...])
        dc_ref[own] = dc
        head_ref[m] = dc[0:8]
        acc[0] += jnp.sum(dza.astype(F32), axis=0, keepdims=True)
        acc[1] += jnp.sum(dzx.astype(F32), axis=0, keepdims=True)
        acc[2] += jnp.sum(dla * rate, axis=0, keepdims=True)
    sums_ref[...] = jnp.zeros_like(sums_ref)
    sums_ref[0:1] = acc[0]
    sums_ref[1:2] = acc[1]
    sums_ref[2:3] = -acc[2] * vec_ref[8:9]


def conv_bwd_kernel(s_ref, dc_ref, head_ref, vb_ref, yb_ref, dyb_ref, vec_ref, w_ref,
                    dvb_ref, keep_ref, swap_ref, sums_ref):
    batches = 2
    ext = vb_ref.shape[0] // batches
    toks = ext - HALO
    lanes = vb_ref.shape[1]
    start = s_ref[ME] * toks
    acc = [jnp.zeros((1, lanes), F32) for _ in range(5)]
    products = []
    for m in range(batches):
        own = slice(m * toks, (m + 1) * toks)
        vb = vb_ref[m * ext : (m + 1) * ext]
        dc = dc_ref[own]
        longer = jnp.concatenate([dc, head_ref[m]], axis=0)
        place = start + lax.broadcasted_iota(jnp.int32, dc.shape, 0)
        place_long = start + lax.broadcasted_iota(jnp.int32, longer.shape, 0)
        dvb = jnp.zeros(dc.shape, F32)
        for k in range(4):
            masked = jnp.where(conv_mask(place_long, s_ref[m], k), longer, 0.0)
            dvb = dvb + vec_ref[k : k + 1] * rolled(masked, -k)[:toks]
            prior = rolled(vb, k)[HALO:]
            acc[k] += jnp.sum(jnp.where(conv_mask(place, s_ref[m], k), dc * prior, 0.0), axis=0, keepdims=True)
        acc[4] += jnp.sum(dc, axis=0, keepdims=True)
        dvb16 = dvb.astype(BF16)
        dvb_ref[own] = dvb16
        products.append(dvb16.astype(F32) * vb[HALO:] + dyb_ref[own].astype(F32) * yb_ref[own])
    sums_ref[...] = jnp.zeros_like(sums_ref)
    for k in range(5):
        sums_ref[k : k + 1] = acc[k]
    side = inner_rows(jnp.concatenate(products, axis=0))
    width = keep_ref.shape[2]
    total = batches * toks
    for r, mine, other in chunk_places(s_ref):
        for ref, block in ((swap_ref, other), (keep_ref, mine)):
            here = lane_block(block, width)
            got = mm(dyb_ref[...], w_ref[:lanes, here]) + mm(dvb_ref[...], w_ref[lanes : 2 * lanes, here])
            ref[r, :total] = got.astype(BF16)
            ref[r, total:] = side


def dp_pairs(along_x, by):
    pairs = []
    for y in range(SIDE):
        for x in range(SIDE):
            there = (y * SIDE + (x + by) % SIDE) if along_x else ((y + by) % SIDE * SIDE + x)
            pairs.append((y * SIDE + x, there))
    return pairs


def send(value, along_x, by):
    return lax.ppermute(value, "dp", dp_pairs(along_x, by))


def send_z(value, by):
    return lax.ppermute(value, "mp", [(z * 2 + c, (z + by) % SIDE * 2 + c) for z in range(SIDE) for c in range(2)])


def swap_cores(value):
    return lax.ppermute(value, "mp", [(i, i ^ 1) for i in range(2 * SIDE)])


def relay(value):
    pairs = [(z * 2 + c, (z + (1, -1)[c]) % SIDE * 2 + c) for z in range(SIDE) for c in range(2)]
    return lax.ppermute(value, "mp", pairs)


def gather_mp(value, core):
    low, high = send_z(value, 1), send_z(value, -1)
    three = jnp.stack([value, low, high])
    far = relay(jnp.where(core == 0, low, high))
    return three, far, swap_cores(three), swap_cores(far)


def reduce_mp(keep, swap, core):
    both = keep.astype(F32) + swap_cores(swap).astype(F32)
    passed = relay(both[2].astype(BF16)).astype(F32)
    low = send_z((both[1] + jnp.where(core == 0, passed, 0.0)).astype(BF16), 1)
    high = send_z((both[3] + jnp.where(core == 1, passed, 0.0)).astype(BF16), -1)
    return both[0], low, high


def exchange_z(chunks):
    lines = [[z * 2 + c for z in range(SIDE)] for c in range(2)]
    return lax.all_to_all(chunks, "mp", 0, 0, axis_index_groups=lines, tiled=True)


def exchange(chunks, axis):
    return lax.all_to_all(chunks, axis, 0, 0, tiled=True)


def to_all(value, axis):
    return exchange(jnp.broadcast_to(value[None], (lax.axis_size(axis),) + value.shape), axis)


def inner_column(rows):
    flat = rows.T
    return flat[:, 0:1] + flat[:, 1:2]


def dn2_sum_kernel(got_ref, rho_ref, dn2_ref, inner_ref, many_ref):
    toks = dn2_ref.shape[0]
    total = got_ref[0].astype(F32)
    for j in range(1, got_ref.shape[0]):
        total = total + got_ref[j].astype(F32)
    dn2_ref[...] = total[:toks]
    inner_ref[...] = inner_column(total[toks:]) / rho_ref[...]
    low = total[:toks].astype(BF16)
    for j in range(many_ref.shape[0]):
        many_ref[j] = low


def finish_kernel(both_ref, low_ref, high_ref, x_ref, cot_ref, x2_ref, dn2_ref, rho1_ref, rho2_ref, inner2_ref,
                  gains_ref, conv_ref, gate_ref, grad_ref, pack_ref, *, batches, full):
    total, width = x_ref.shape
    toks = total // batches
    ext = rho1_ref.shape[0] // batches
    got = both_ref[...] + low_ref[...].astype(F32) + high_ref[...].astype(F32)
    dn1, dn2, x2 = got[:total], dn2_ref[...], x2_ref[...]
    x = x_ref[...].astype(F32)
    rho1 = jnp.concatenate([rho1_ref[m * ext + HALO : (m + 1) * ext] for m in range(batches)], axis=0)
    rho2 = rho2_ref[...]
    inner1 = inner_column(got[total:]) / rho1
    gx2 = (cot_ref[...].astype(F32) + rho2 * gains_ref[1:2] * dn2
           - x2 * (rho2 * rho2 * rho2 / full * inner2_ref[...]))
    grad_ref[...] = gx2 + rho1 * gains_ref[0:1] * dn1 - x * (rho1 * rho1 * rho1 / full * inner1)
    gain_grads = (jnp.sum(dn1 * x * rho1, axis=0, keepdims=True), jnp.sum(dn2 * x2 * rho2, axis=0, keepdims=True))
    pack_ref[...] = jnp.zeros_like(pack_ref)
    deep = pack_ref.shape[0]
    sums = jnp.concatenate([conv_ref[:5], gate_ref[:3]], axis=0)
    size = sums.shape[1] // 2
    for i in range(deep):
        few = size // deep
        for j in range(2):
            at = j * size + i * few
            pack_ref[i, 8 * j : 8 * j + 8, :few] = sums[:, at : at + few]
        for k, row in enumerate(gain_grads):
            pack_ref[i, 16 + k : 17 + k, : width // deep] = row[:, i * (width // deep) : (i + 1) * (width // deep)]


def small_out_kernel(got_ref, taps_ref, shift_ref, rate_ref, input_ref, decay_ref, one_ref, two_ref):
    total = got_ref[0]
    for i in range(1, got_ref.shape[0]):
        total = total + got_ref[i]
    few = shift_ref.shape[1]
    for j in range(2):
        for k in range(4):
            taps_ref[k, j : j + 1, :] = total[8 * j + k : 8 * j + k + 1, :few]
        for k, ref in enumerate((shift_ref, rate_ref, input_ref, decay_ref)):
            ref[j : j + 1, :] = total[8 * j + 4 + k : 8 * j + 5 + k, :few]
    one_ref[...] = total[16:17, : one_ref.shape[1]]
    two_ref[...] = total[17:18, : two_ref.shape[1]]


def late_kernel(dvb_ref, n1_ref, c_ref, dza_ref, dzx_ref, out_ref):
    deep, _, rows = out_ref.shape
    lanes = dvb_ref.shape[1]
    size = lanes // 2
    few = size // deep
    for i in range(0, deep, SIDE):
        got = mm_tn(dvb_ref[...], n1_ref[:, i * rows : (i + SIDE) * rows]).astype(BF16)
        for d in range(SIDE):
            out_ref[i + d, :lanes] = got[:, d * rows : (d + 1) * rows]
    out_ref[:, lanes:] = jnp.zeros((deep, out_ref.shape[1] - lanes, rows), BF16)
    for kind, ref in enumerate((dza_ref, dzx_ref)):
        both = mm_tn(c_ref[...], ref[...])
        for j in range(2):
            k = 2 * kind + j
            block = both[j * size : (j + 1) * size, j * size : (j + 1) * size].astype(BF16)
            for i in range(deep):
                part = block[i * few : (i + 1) * few]
                out_ref[i, lanes + 16 * k : lanes + 16 * k + few] = part[:, :rows]
                at = lanes + 64 + 16 * (k // 2)
                here = slice(64 * (k % 2), 64 * (k % 2) + size - rows)
                out_ref[i, at : at + few, here] = part[:, rows:]


def late_out_kernel(got_ref, value_ref, rate_ref, input_ref):
    lanes, rows = value_ref.shape
    few, _, size = rate_ref.shape
    total = got_ref[0].astype(F32)
    for i in range(1, got_ref.shape[0]):
        total = total + got_ref[i].astype(F32)
    value_ref[...] = total[:lanes]
    for kind, ref in enumerate((rate_ref, input_ref)):
        for j in range(2):
            k = 2 * kind + j
            at = lanes + 16 * k
            ref[:, j, :rows] = total[at : at + few]
            at = lanes + 64 + 16 * (k // 2)
            ref[:, j, rows:] = total[at : at + few, 64 * (k % 2) : 64 * (k % 2) + size - rows]


def early_out_kernel(got_ref, out_ref, branch_ref):
    lanes = out_ref.shape[0]
    out_ref[...] = got_ref[:lanes].astype(F32)
    branch_ref[...] = got_ref[lanes:].astype(F32)


def beside(at):
    return at + 1 - 2 * (at % 2)


def across(at):
    return SIDE - 1 - at


def send_to(value, along_x, partner):
    pairs = []
    for y in range(SIDE):
        for x in range(SIDE):
            there = (y * SIDE + partner(x)) if along_x else (partner(y) * SIDE + x)
            pairs.append((y * SIDE + x, there))
    return lax.ppermute(value, "dp", pairs)


def at_of(s_ref, along_x):
    return s_ref[COL_X if along_x else ROW_Y]


def partners_of(one_set):
    return (beside, across) if one_set[3] is beside else (across, beside)


def whole_spec(dims):
    return pl.BlockSpec(dims, lambda i: (0,) * len(dims))


def half_spec(units, wide, index):
    return pl.BlockSpec((units, wide), lambda i: (0, index))


def call_whole(name, kernel, outs, args, specs=None, scratch=(), ties=()):
    ins = [SCALARS if v.dtype == jnp.int32 else whole_spec(v.shape) for v in args]
    for k, spec in (specs or {}).items():
        ins[k] = spec
    return call(kernel, outs, ins, args, grid=(1,), out_specs=[whole_spec(o.shape) for o in outs], scratch=scratch,
                name=name, ties=ties)


def halving_one(name, scalars, group, wide, ties=()):
    operands, sets = group

    def kernel(s_ref, *refs):
        ins, outs = refs[: len(operands)], refs[len(operands) :]
        for one_set, out_ref in zip(sets, outs):
            first, second = partners_of(one_set)
            there = first(at_of(s_ref, one_set[2]))
            out_ref[:, :wide] = one_set[0](ins, there).astype(BF16)
            out_ref[:, wide:] = one_set[0](ins, second(there)).astype(BF16)

    outs = [shape((t[1], 2 * wide), BF16) for t in sets]
    sent = call_whole(name, kernel, outs, (scalars, *operands), ties=ties)
    return sent, [send_to(v, t[2], partners_of(t)[0]) for v, t in zip(sent, sets)]


def halving_two(name, scalars, group, wide, got, ties=()):
    operands, sets = group

    def kernel(s_ref, *refs):
        ins, got, outs = refs[: len(operands)], refs[len(operands) : -len(sets)], refs[-len(sets) :]
        for one_set, got_ref, out_ref in zip(sets, got, outs):
            there = partners_of(one_set)[1](at_of(s_ref, one_set[2]))
            out_ref[...] = (one_set[0](ins, there) + got_ref[...].astype(F32)).astype(BF16)

    outs = [shape((t[1], wide), BF16) for t in sets]
    specs = {1 + len(operands) + k: half_spec(t[1], wide, 1) for k, t in enumerate(sets)}
    sent = call_whole(name, kernel, outs, (scalars, *operands, *got), specs, ties=ties)
    return sent, [send_to(v, t[2], partners_of(t)[1]) for v, t in zip(sent, sets)]


def halving_three(name, scalars, group, wide, got_one, got_two, ties=()):
    size = wide // SIDE
    operands, sets = group
    tall = [sum(t[1] for t in sets if t[2] == along_x) for along_x in (False, True)]
    count = len(operands)

    def kernel(s_ref, *refs):
        ins, ones, twos = refs[:count], refs[count : count + len(sets)], refs[count + len(sets) : -2 * SIDE - 1]
        outs, held = refs[-2 * SIDE - 1 : -1], refs[-1]
        start = [0, 0]
        for (chunk, units, along_x, _), one, two in zip(sets, ones, twos):
            held[:units] = chunk(ins, at_of(s_ref, along_x)) + one[...].astype(F32) + two[...].astype(F32)
            here = slice(start[along_x], start[along_x] + units)
            start[along_x] += units
            for d in range(SIDE):
                ref = outs[SIDE * along_x + d]
                at = (at_of(s_ref, not along_x) + d) % SIDE
                ref[here] = held[:units, lane_block(at, size)].astype(ref.dtype)

    outs = [shape((tall[k], size), BF16 if d else F32) for k in range(2) for d in range(SIDE)]
    specs = {1 + count + k: half_spec(t[1], wide, 0) for k, t in enumerate(sets)}
    parts = call_whole(name, kernel, outs, (scalars, *operands, *got_one, *got_two), specs,
                       [pltpu.VMEM((max(t[1] for t in sets), wide), F32)], ties)
    return [parts[SIDE * k + d] if d == 0 else send(parts[SIDE * k + d], not k, d) for k in range(2) for d in range(SIDE)]


def block_diagonal(blocks):
    count, size = blocks.shape[0], blocks.shape[1]
    rows = [jnp.pad(blocks[j], ((0, 0), (j * size, (count - 1 - j) * size))) for j in range(count)]
    return jnp.concatenate(rows, axis=0)


def body(inputs, cotangent, row_split, first_gain, branch_weight, value_weight, conv_weight, conv_bias,
         rate_blocks, input_blocks, rate_bias, input_bias, decay_param, out_weight, second_gain,
         gate_weight, up_weight, down_weight):
    batches, toks, width = inputs.shape
    parts = lax.axis_size("mp")
    deep = lax.axis_size("dp")
    full = width * parts
    blocks, size = rate_blocks.shape[0], rate_blocks.shape[1]
    lanes = blocks * size
    rows = branch_weight.shape[0]
    units = gate_weight.shape[1]
    total = batches * toks
    ext = toks + HALO
    me = lax.axis_index("dp")
    at_mp = lax.axis_index("mp")
    core = at_mp % 2
    scalars = jnp.concatenate(
        [row_split, jnp.stack([me, me // SIDE, me % SIDE, at_mp // 2, core, jnp.zeros_like(me)])]).astype(jnp.int32)

    w_rec = lax.all_gather(jnp.concatenate([branch_weight.T, value_weight.T, out_weight], axis=0), "dp")
    w_ffn = lax.all_gather(jnp.stack([gate_weight, up_weight, down_weight.T]), "dp")

    decay = decay_param.reshape(1, lanes).astype(F32)
    vectors = jnp.concatenate(
        [conv_weight.reshape(4, lanes).astype(F32), conv_bias.reshape(1, lanes).astype(F32),
         rate_bias.reshape(1, lanes).astype(F32), input_bias.reshape(1, lanes).astype(F32),
         8.0 * jax.nn.softplus(decay), 8.0 * jax.nn.sigmoid(decay), jnp.zeros((7, lanes), F32)], axis=0)
    rate_mat = block_diagonal(rate_blocks)
    input_mat = block_diagonal(input_blocks)

    pairs = [(i, i + 1) for i in range(deep - 1)]
    before = lax.ppermute(inputs[:, toks - HALO :], "dp", pairs)
    gains = jnp.concatenate([first_gain[None], second_gain[None], jnp.zeros((HALO - 2, width), BF16)], axis=0)
    payload = jnp.concatenate([jnp.concatenate([before, inputs], axis=1).reshape(batches * ext, width), gains], axis=0)
    x_parts = gather_mp(payload, core)
    n1, n1_own, rho1, gain_rows = call(
        norm_one_kernel,
        [shape((batches * ext, full), BF16), shape((total, full), BF16), shape((batches * ext, 1)), shape((HALO, full))],
        [SCALARS] + [WHOLE] * 4, (scalars, *x_parts),
        scratch=[pltpu.VMEM((batches * ext, full), BF16)], name="norm_one")
    cot_parts = gather_mp(cotangent.reshape(total, width), core)

    grown = shape((total, lanes))

    def full_spec(dims):
        return pl.BlockSpec(dims, lambda i: (0,) * len(dims))

    w_rec, yb, vb, c, rate, gate, a, prod, state, last = call(
        rec_fwd_kernel,
        [shape((3 * lanes, full), BF16), grown, shape((batches * ext, lanes)), shape((total, lanes), BF16)]
        + [grown] * 5 + [shape((8, lanes))],
        [SCALARS] + [WHOLE] * 5,
        (scalars, n1, w_rec, vectors, rate_mat, input_mat), name="rec_fwd", ties=cot_parts)
    ends = to_all(last, "dp")
    chunk = shape((SIDE, total, width), BF16)
    chunk_long = shape((SIDE, total + HALO, width), BF16)
    def with_weights(kernel, outs, args, w_at, blocks_at, name, ties=()):
        ins = [SCALARS if a.dtype == jnp.int32 else full_spec(a.shape) for a in args]
        ins[w_at] = pl.BlockSpec((blocks_at[1] * lanes, full), lambda i: (blocks_at[0], 0))
        return call(kernel, outs, ins, args, grid=(1,), out_specs=[full_spec(o.shape) for o in outs],
                    name=name, ties=ties)

    h, carry, o, keep, swap = with_weights(
        rec_out_kernel, [grown, shape((8, lanes)), shape((total, lanes), BF16), chunk, chunk],
        (scalars, ends, prod, state, yb, w_rec), 5, (2, 1), "rec_out")
    x_own = inputs.reshape(total, width).astype(F32)
    both, low, high = reduce_mp(keep, swap, core)
    x2 = x_own + (both + low.astype(F32) + high.astype(F32))
    x2_parts = gather_mp(x2.astype(BF16), core)

    steps = 3
    cols = units // steps
    n2, x2_full, rho2, cot_full = call(
        norm_two_kernel,
        [shape((total, full), BF16)] * 2 + [shape((total, 1)), shape((total, full), BF16)], [SCALARS] + [WHOLE] * 9,
        (scalars, *x2_parts, *cot_parts, gain_rows), name="norm_two")
    hid, dgt, dup, part_o, keep, swap = call(
        ffn_kernel,
        [shape((total, units), BF16)] * 3 + [shape((total, full), BF16), chunk_long, chunk_long],
        [SCALARS, full_spec(n2.shape), full_spec(n2.shape),
         pl.BlockSpec((deep, 3, rows, cols), lambda g: (0, 0, 0, g))],
        (scalars, n2, cot_full, w_ffn),
        grid=(steps,),
        out_specs=[pl.BlockSpec((total, cols), lambda g: (0, g))] * 3
        + [full_spec((total, full)), full_spec(chunk_long.shape), full_spec(chunk_long.shape)],
        scratch=[pltpu.VMEM((total, full), F32), pltpu.VMEM((total, full), F32), pltpu.VMEM((total, cols), F32)],
        name="ffn")

    def row_lanes(ref, at):
        return ref[:, lane_block(at, SIDE * rows)]

    def column_lanes(ref, at):
        return jnp.concatenate([ref[:, lane_block(y * SIDE + at, rows)] for y in range(SIDE)], axis=1)

    mid, low = units // 2, units // 4

    def ffn_set(along_x, second):
        lanes_of = column_lanes if along_x else row_lanes
        main = slice(second * mid, (second + 1) * mid)
        part = slice((2 * along_x + second) * low, (2 * along_x + second + 1) * low)

        def chunk(refs, at):
            n2_ref, cot_ref, hid_ref = refs[0], refs[1], refs[4]
            grad_ref = refs[3] if along_x else refs[2]
            return jnp.concatenate(
                [mm_tn(grad_ref[:, main], lanes_of(n2_ref, at)), mm_tn(hid_ref[:, part], lanes_of(cot_ref, at))], axis=0)

        return chunk, mid + low, along_x, across if second else beside

    wide = SIDE * rows
    ffn_group = ((n2, cot_full, dgt, dup, hid),
                 [ffn_set(along_x, second) for along_x in (False, True) for second in (False, True)])
    dn2_parts = (keep.astype(F32) + swap_cores(swap).astype(F32)).astype(BF16)
    ffn_one, ffn_got_one = halving_one("ffn_grad_one", scalars, ffn_group, wide, (dn2_parts,))
    layer_part = lax.psum_scatter(part_o, "mp", scatter_dimension=1, tiled=True)
    got = exchange_z(dn2_parts)
    dn2, inner2, dn2_many = call(
        dn2_sum_kernel, [shape((total, width)), shape((total, 1)), shape((SIDE, total, width), BF16)], [WHOLE] * 2,
        (got, rho2), name="dn2_sum", ties=(ffn_one[0],))
    dn2_line = exchange_z(dn2_many)

    gr, dyb, adj, adj_prod, first = with_weights(
        rec_bwd_kernel,
        [shape((total, full), BF16), shape((total, lanes), BF16), grown, grown, shape((deep, 8, lanes))],
        (scalars, dn2_line, swap_cores(dn2_line), x2_full, cot_full, gain_rows, rho2, inner2, w_rec, yb, h, a, prod),
        8, (2, 1), "rec_bwd")

    starts = exchange(first, "dp")

    def early_kernel(o_ref, gr_ref, dyb_ref, n1_ref, out_ref):
        for k, (left, right) in enumerate(((o_ref, gr_ref), (dyb_ref, n1_ref))):
            units_at = slice(k * lanes, (k + 1) * lanes)
            for i in range(0, deep, SIDE):
                got = mm_tn(left[...], right[:, i * rows : (i + SIDE) * rows]).astype(BF16)
                for d in range(SIDE):
                    out_ref[i + d, units_at] = got[:, d * rows : (d + 1) * rows]

    early = call(early_kernel, [shape((deep, 2 * lanes, rows), BF16)], [WHOLE] * 4, (o, gr, dyb, n1_own),
                 name="early_grad", ties=tuple(ffn_got_one))[0]
    ffn_two, ffn_got_two = halving_two("ffn_grad_two", scalars, ffn_group, wide, ffn_got_one, (early,))
    early = lax.psum_scatter(early.reshape(-1, rows), "dp", scatter_dimension=0, tiled=True)

    dza, dzx, dc, head, sums_gate = call(
        gate_bwd_kernel,
        [shape((total, lanes), BF16)] * 2 + [grown, shape((batches, 8, lanes)), shape((8, lanes))],
        [SCALARS] + [WHOLE] * 12,
        (scalars, starts, adj, adj_prod, a, h, carry, c, rate, gate, vectors, rate_mat, input_mat),
        name="gate_bwd", ties=(ffn_two[0],))
    following = lax.ppermute(head, "dp", [(i + 1, i) for i in range(deep - 1)])
    dvb, keep, swap, sums_conv = with_weights(
        conv_bwd_kernel,
        [shape((total, lanes), BF16), chunk_long, chunk_long, shape((8, lanes))],
        (scalars, dc, following, vb, yb, dyb, vectors, w_rec), 7, (0, 2), "conv_bwd")
    late = call(late_kernel, [shape((deep, lanes + 96, rows), BF16)], [WHOLE] * 5, (dvb, n1_own, c, dza, dzx),
                name="late_grad")[0]
    keep, ffn_got_two = lax.optimization_barrier((keep, ffn_got_two))
    late_got = exchange(late, "dp")
    both, below, above = reduce_mp(keep, swap, core)
    grad_sums = halving_three("ffn_grad_three", scalars, ffn_group, wide, ffn_got_one, ffn_got_two, (late,))
    layer_out = (x2 + layer_part.astype(F32)).astype(BF16)
    small_gains = jnp.stack([first_gain, second_gain]).astype(F32)
    input_grad, pack = call(
        functools.partial(finish_kernel, batches=batches, full=full),
        [shape((total, width)), shape((deep, 24, rows))], [WHOLE] * 13,
        (both, below, above, inputs.reshape(total, width), cotangent.reshape(total, width), x2, dn2, rho1, rho2, inner2,
         small_gains, sums_conv, sums_gate), name="finish")
    few = size // deep
    pair = shape((blocks, few))
    pack, late_got = lax.optimization_barrier((pack, late_got))
    value_grad, rate_g, input_g = call(
        late_out_kernel, [shape((lanes, rows))] + [shape((few, blocks, size))] * 2, [WHOLE], (late_got,),
        name="late_out")
    taps, shift, rate_b, input_b, decay_g, gain_a, gain_b = call(
        small_out_kernel, [shape((4, blocks, few)), pair, pair, pair, pair] + [shape((1, width // deep))] * 2, [WHOLE],
        (exchange(pack, "dp"),), name="small_out")
    out_grad, branch_grad = call(early_out_kernel, [shape((lanes, rows))] * 2, [WHOLE], (early,), name="early_out")

    def ffn_out_kernel(*refs):
        outs = refs[2 * SIDE :]
        for k in range(2):
            for second in range(2):
                at = second * (mid + low)
                sums = [sum(ref[there].astype(F32) for ref in refs[SIDE * k : SIDE * k + SIDE])
                        for there in (slice(at, at + mid), slice(at + mid, at + mid + low))]
                outs[k][:, second * mid : (second + 1) * mid] = sums[0].T
                outs[2][(2 * k + second) * low : (2 * k + second + 1) * low] = sums[1]

    gate_grad, up_grad, down = call(
        ffn_out_kernel, [shape((rows, units))] * 2 + [shape((units, rows))], [WHOLE] * (2 * SIDE),
        grad_sums, name="ffn_out", ties=(pack, value_grad, out_grad))

    return (
        layer_out.reshape(batches, toks, width), input_grad.reshape(batches, toks, width),
        gain_a.reshape(-1), branch_grad.T, value_grad.T, taps, shift, rate_g.transpose(1, 0, 2),
        input_g.transpose(1, 0, 2), rate_b, input_b, decay_g,
        out_grad, gain_b.reshape(-1), gate_grad, up_grad, down,
    )


def solution(mesh):
    placed = (
        P(None, "dp", "mp"), P(None, "dp", "mp"), P(), P("mp"), P("dp", "mp"), P("dp", "mp"),
        P(None, "mp", None), P("mp", None), P("mp", None, None), P("mp", None, None), P("mp", None),
        P("mp", None), P("mp", None), P("mp", "dp"), P("mp"), P("dp", "mp"), P("dp", "mp"), P("mp", "dp"),
    )
    given = (
        P(None, "dp", "mp"), P(None, "dp", "mp"), P(("mp", "dp")), P("dp", "mp"), P("dp", "mp"),
        P(None, "mp", "dp"), P("mp", "dp"), P("mp", "dp", None), P("mp", "dp", None), P("mp", "dp"),
        P("mp", "dp"), P("mp", "dp"), P("mp", "dp"), P(("mp", "dp")), P("dp", "mp"), P("dp", "mp"), P("mp", "dp"),
    )
    return jax.shard_map(body, mesh=mesh, in_specs=placed, out_specs=given, check_vma=False)
```
